128 devices in a mesh: section: 2 (over core), seq: 4 (over y), fsdp: 16 (over x, z).
Axes of the slice: x: 4, y: 4, z: 4, core: 2. Of those that a mesh axis runs over, the one named last changes fastest.
Arguments:
- tokens_in: bfloat16 [2, 16, 256, 768], P(None, 'fsdp', 'seq'), may hold values from -6 to 6
- cotangent: bfloat16 [2, 16, 256, 768], P(None, 'fsdp', 'seq'), may hold values from -6 to 6
- positions: int32 [2, 16, 256], P(None, 'fsdp', 'seq'), may hold values from 0 to 511, as said below
- first_gain: bfloat16 [2, 768], P('section', 'fsdp'), may hold values from 0.5 to 1.5
- first_bias: bfloat16 [2, 768], P('section', 'fsdp'), may hold values from -1.5 to 1.5
- second_gain: bfloat16 [2, 768], P('section', 'fsdp'), may hold values from 0.5 to 1.5
- second_bias: bfloat16 [2, 768], P('section', 'fsdp'), may hold values from -1.5 to 1.5
- qkv_weight: bfloat16 [2, 768, 2304], P('section', 'fsdp'), may hold values from -0.21875 to 0.21875
- qkv_bias: bfloat16 [2, 2304], P('section', 'fsdp'), may hold values from -1.5 to 1.5
- dense_weight: bfloat16 [2, 768, 768], P('section', 'fsdp'), may hold values from -1.75 to 1.75
- dense_bias: bfloat16 [2, 768], P('section', 'fsdp'), may hold values from -1.5 to 1.5
- expand_weight: bfloat16 [2, 768, 3072], P('section', 'fsdp'), may hold values from -0.21875 to 0.21875
- expand_bias: bfloat16 [2, 3072], P('section', 'fsdp'), may hold values from -1.5 to 1.5
- shrink_weight: bfloat16 [2, 3072, 768], P('section', 'fsdp'), may hold values from -0.15625 to 0.15625
- shrink_bias: bfloat16 [2, 768], P('section', 'fsdp'), may hold values from -1.5 to 1.5
Outputs:
- layer_out: bfloat16 [2, 2, 16, 256, 768], P('section', None, 'fsdp', 'seq')
- input_grad: bfloat16 [2, 2, 16, 256, 768], P('section', None, 'fsdp', 'seq')
- first_gain_grad: float32 [2, 768], P('section', 'fsdp')
- first_bias_grad: float32 [2, 768], P('section', 'fsdp')
- second_gain_grad: float32 [2, 768], P('section', 'fsdp')
- second_bias_grad: float32 [2, 768], P('section', 'fsdp')
- qkv_weight_grad: float32 [2, 768, 2304], P('section', 'fsdp')
- qkv_bias_grad: float32 [2, 2304], P('section', 'fsdp')
- dense_weight_grad: float32 [2, 768, 768], P('section', 'fsdp')
- dense_bias_grad: float32 [2, 768], P('section', 'fsdp')
- expand_weight_grad: float32 [2, 768, 3072], P('section', 'fsdp')
- expand_bias_grad: float32 [2, 3072], P('section', 'fsdp')
- shrink_weight_grad: float32 [2, 3072, 768], P('section', 'fsdp')
- shrink_bias_grad: float32 [2, 768], P('section', 'fsdp')
The draws below stay inside these ranges and needn't reach their ends.
Inputs may be any that keep to these rules, and one draw needn't show every extreme that they name: `positions`: in every sequence the position of token i is 2 i or 2 i + 1.
All inputs are finite; a program needn't handle non-finite values.
Results may differ from the reference program's by a relative error of at most 0.02.
Values may be sent and summed in bfloat16 or wider, within the bound.
A program may use at most 128 MiB of HBM per device.

```python
import math
import jax
import jax.numpy as jnp
from jax import lax

D = 768
HEADS = 12
FF = 3072
HD = 64
ROT = 16
MICRO = 2
LEN = 256
SEQS = 16


def draw_positions(key, part):
    key = jax.random.fold_in(key, 7)
    offsets = jax.random.randint(key, (MICRO, SEQS, LEN), 0, 2)
    offsets = offsets.at[0, 0, 0].set(0)
    offsets = offsets.at[0, 0, LEN - 1].set(1)
    doubled = jnp.arange(LEN, dtype=jnp.int32) * 2
    return (doubled + offsets).astype(jnp.int32)


def block_scale(stream_key, extent, cuts, smallest, top_value):
    def one(position, blocks):
        steps = jax.random.uniform(jax.random.fold_in(jax.random.fold_in(stream_key, 6), position), (blocks,), jnp.float32, smallest / len(cuts), top_value / len(cuts))
        return jnp.repeat(jnp.exp(steps), extent[position] // blocks).reshape((-1,) + (1,) * (len(extent) - position - 1))

    loudness = one(*cuts[0])
    for cut in cuts[1:]:
        loudness = loudness * one(*cut)
    return loudness


def scatter_about(own_key, extent, scale, bound, cuts=(), kind=jnp.bfloat16):
    values = scale * jax.random.normal(own_key, extent, jnp.float32)
    if cuts:
        values = values * block_scale(own_key, extent, cuts, -0.22, 0.18)
    return jnp.clip(values, -bound, bound).astype(kind)


def setup_inputs(seed: int = 0) -> dict:
    keys = jax.random.split(jax.random.key(seed), 16)
    return {
        "tokens_in": scatter_about(keys[0], (MICRO, SEQS, LEN, D), 1.0, 6.0, ((1, 16), (2, 4))),
        "cotangent": scatter_about(keys[1], (MICRO, SEQS, LEN, D), 1.0, 6.0, ((1, 16), (2, 4))),
        "positions": draw_positions(jax.random.fold_in(keys[15], 71), 0),
        "first_gain": jnp.clip(1.0 + 0.1 * jax.random.normal(keys[3], (2, D), jnp.float32), 0.5, 1.5).astype(jnp.bfloat16),
        "first_bias": scatter_about(keys[4], (2, D), 0.3, 1.5, ((0, 2), (1, 16))),
        "second_gain": jnp.clip(1.0 + 0.1 * jax.random.normal(keys[5], (2, D), jnp.float32), 0.5, 1.5).astype(jnp.bfloat16),
        "second_bias": scatter_about(keys[6], (2, D), 0.3, 1.5, ((0, 2), (1, 16))),
        "qkv_weight": scatter_about(keys[7], (2, D, 3 * D), D ** -0.5, 0.21875, ((0, 2), (1, 16))),
        "qkv_bias": scatter_about(keys[8], (2, 3 * D), 0.3, 1.5, ((0, 2), (1, 16))),
        "dense_weight": scatter_about(keys[9], (2, D, D), (D // 64) ** -0.5, 1.75, ((0, 2), (1, 16))),
        "dense_bias": scatter_about(keys[10], (2, D), 0.3, 1.5, ((0, 2), (1, 16))),
        "expand_weight": scatter_about(keys[11], (2, D, FF), D ** -0.5, 0.21875, ((0, 2), (1, 16))),
        "expand_bias": scatter_about(keys[12], (2, FF), 0.3, 1.5, ((0, 2), (1, 16))),
        "shrink_weight": scatter_about(keys[13], (2, FF, D), (FF // 2) ** -0.5, 0.15625, ((0, 2), (1, 16))),
        "shrink_bias": scatter_about(keys[14], (2, D), 0.3, 1.5, ((0, 2), (1, 16))),
    }


@jax.custom_vjp
def low(v):
    return lax.optimization_barrier(v.astype(jnp.bfloat16)).astype(jnp.float32)

@jax.custom_vjp
def low_back(v):
    return v

def low_keep(v):
    return (low(v), None)

def low_pass(kept, grad):
    return (grad,)

def back_keep(v):
    return (v, None)

def back_low(kept, grad):
    return (low(grad),)
low.defvjp(low_keep, low_pass)
low_back.defvjp(back_keep, back_low)

def layer_norm(values, scaling, offset_vec):
    center = values - lax.optimization_barrier(jnp.mean(values, axis=-1, keepdims=True))
    spread = lax.optimization_barrier(jnp.mean(center * center, axis=-1, keepdims=True))
    return center * lax.rsqrt(spread + 1e-05) * scaling + offset_vec

def rotary_tables(places, rot_width):
    half_width = rot_width // 2
    exponent = jnp.arange(half_width, dtype=jnp.float32) * (2.0 / rot_width)
    frequency = jnp.exp(-math.log(10000.0) * exponent)
    angles = places.astype(jnp.float32)[..., None] * frequency
    angles = jnp.concatenate([angles, angles], axis=-1)
    return (jnp.cos(angles), jnp.sin(angles))

def rotate(head_vals, cosine, sine, rot_width):
    rotated_part = head_vals[..., :rot_width]
    half_width = rot_width // 2
    turned = jnp.concatenate([-rotated_part[..., half_width:], rotated_part[..., :half_width]], axis=-1)
    rotated = rotated_part * cosine + turned * sine
    return jnp.concatenate([rotated, head_vals[..., rot_width:]], axis=-1)

def matmul_high(left_side, right_side):
    return jnp.einsum('gld,de->gle', left_side, right_side, precision=lax.Precision.HIGHEST)

def block_layer(values, places, params):
    first_gain, first_bias, second_gain, second_bias, qkv_weight, qkv_bias, dense_weight, dense_bias, expand_weight, expand_bias, shrink_weight, shrink_bias = params
    groups, length, width = values.shape
    first = low(layer_norm(values, first_gain, first_bias))
    joined = low_back(matmul_high(first, qkv_weight) + qkv_bias).reshape(groups, length, 3, HEADS, HD)
    cosine, sine = rotary_tables(places, ROT)
    cosine = cosine[:, :, None, :]
    sine = sine[:, :, None, :]
    queries = low(low_back(rotate(joined[:, :, 0], cosine, sine, ROT)))
    key_heads = low(low_back(rotate(joined[:, :, 1], cosine, sine, ROT)))
    value_heads = low(low_back(joined[:, :, 2]))
    scores = jnp.einsum('gqhd,gkhd->ghqk', queries, key_heads, precision=lax.Precision.HIGHEST)
    scores = low_back(scores * HD ** (-0.5))
    causal = jnp.arange(length)[:, None] >= jnp.arange(length)[None, :]
    scores = jnp.where(causal, scores, -1e+30)
    row_max = lax.optimization_barrier(jnp.max(scores, axis=-1, keepdims=True))
    powers = jnp.exp(scores - row_max)
    attn_probs = powers / lax.optimization_barrier(jnp.sum(powers, axis=-1, keepdims=True))
    context = jnp.einsum('ghqk,gkhd->gqhd', low(attn_probs), value_heads, precision=lax.Precision.HIGHEST)
    context = low(low_back(context)).reshape(groups, length, width)
    attended = matmul_high(context, dense_weight) + dense_bias
    second = low(layer_norm(values, second_gain, second_bias))
    hidden = low_back(matmul_high(second, expand_weight) + expand_bias)
    active = low(jax.nn.gelu(hidden, approximate=False))
    return values + attended + matmul_high(active, shrink_weight) + shrink_bias

def whole_forward(inputs, extra, first_params, second_params, places):
    total_seqs = inputs.shape[0]
    group_size = math.gcd(total_seqs, max(1, 4096 // LEN))
    group_count = total_seqs // group_size
    packed_places = places.reshape(group_count, group_size, LEN)

    def run_layer(params, values):

        def one_piece(packed_pair):
            return jax.checkpoint(block_layer)(packed_pair[0], packed_pair[1], params)
        packed = (values.reshape(group_count, group_size, LEN, D), packed_places)
        return lax.map(one_piece, packed).reshape(values.shape)
    first_out = run_layer(first_params, inputs)
    boundary = low(low_back(first_out)) + extra
    second_out = run_layer(second_params, boundary)
    return (second_out, boundary)

def reference(tokens_in, cotangent, positions, first_gain, first_bias, second_gain, second_bias, qkv_weight, qkv_bias, dense_weight, dense_bias, expand_weight, expand_bias, shrink_weight, shrink_bias):
    params_all = (first_gain, first_bias, second_gain, second_bias, qkv_weight, qkv_bias, dense_weight, dense_bias, expand_weight, expand_bias, shrink_weight, shrink_bias)
    floats = [member.astype(jnp.float32) for member in params_all]
    first_params = tuple((member[0] for member in floats))
    second_params = tuple((member[1] for member in floats))
    inputs = tokens_in.astype(jnp.float32).reshape(-1, LEN, D)
    places = positions.reshape(-1, LEN).astype(jnp.int32)
    extra = jnp.zeros_like(inputs)

    def forward(inputs_now, extra_now, first_now, second_now):
        return whole_forward(inputs_now, extra_now, first_now, second_now, places)
    result, pullback, boundary = jax.vjp(forward, inputs, extra, first_params, second_params, has_aux=True)
    seed_grad = cotangent.astype(jnp.float32).reshape(-1, LEN, D)
    input_part, extra_part, first_grads, second_grads = pullback(seed_grad)
    shape_out = (2, MICRO, SEQS, LEN, D)
    layer_out = jnp.stack([boundary, result]).astype(jnp.bfloat16).reshape(shape_out)
    input_grad = jnp.stack([input_part, extra_part]).astype(jnp.bfloat16).reshape(shape_out)
    stacked = [jnp.stack([first_grads[index], second_grads[index]]) for index in range(12)]
    return (layer_out, input_grad, stacked[0], stacked[1], stacked[2], stacked[3], stacked[4], stacked[5], stacked[6], stacked[7], stacked[8], stacked[9], stacked[10], stacked[11])
```

```python
import math

import jax
import jax.numpy as jnp
import numpy as np
from jax import lax
from jax.experimental import pallas as pl
from jax.experimental.pallas import tpu as pltpu
from jax.sharding import PartitionSpec as P

MESH = pl.DeviceIdType.MESH
F32 = jnp.float32
BF16 = jnp.bfloat16
HD = 64
ROT = 16
WIDTH = 768
TOK = 64
LEN = 256
GROUP = 192
NEAR = (1, 3, 2)
MIB = 1024 * 1024

KINDS = ((48, 576, False), (48, 768, True), (48, 768, False), (16, 128, True))


def ring(value, by):
    return lax.rem(value + by, 4)


def places():
    owner = lax.axis_index("fsdp")
    return owner, lax.div(owner, 4), lax.rem(owner, 4)


def joined(u, v, x_first):
    return u * 4 + v if x_first else v * 4 + u


def remote(src, dst, send, recv, target):
    return pltpu.make_async_remote_copy(
        src_ref=src, dst_ref=dst, send_sem=send, recv_sem=recv, device_id=target, device_id_type=MESH
    )


def greet(targets):
    barrier = pltpu.get_barrier_semaphore()
    for target in targets:
        pl.semaphore_signal(barrier, inc=1, device_id=target, device_id_type=MESH)
    pl.semaphore_wait(barrier, len(targets))


def sheet_peers(x, z):
    return [{"fsdp": ring(x, d) * 4 + z} for d in (1, 2, 3)] + [
        {"fsdp": x * 4 + ring(z, d)} for d in (1, 2, 3)
    ]


def seq_peers(y):
    return [{"seq": ring(y, d)} for d in (1, 2, 3)]


def dot(a, b):
    return jnp.dot(a, b, preferred_element_type=F32)


def dot_nt(a, b):
    return lax.dot_general(a, b, (((1,), (1,)), ((), ())), preferred_element_type=F32)


def dot_tn(a, b):
    return lax.dot_general(a, b, (((0,), (0,)), ((), ())), preferred_element_type=F32)


def gather_kernel(*refs):
    shards, dense = refs[0:4], refs[4]
    wholes, dense_whole = refs[5:9], refs[9]
    send, recv, own_sem, dsend, drecv, csend, crecv = refs[10:]
    layer = lax.axis_index("section")
    y = lax.axis_index("seq")
    owner, x, z = places()
    sibling = {"section": 1 - layer}
    greet(sheet_peers(x, z) + [sibling])

    def slot(t, s):
        rows = KINDS[t][0]
        return wholes[t].at[layer, pl.ds(pl.multiple_of(s * rows, 16), rows), :]

    def band(i):
        return dense_whole.at[layer, pl.ds(pl.multiple_of(i * 48, 16), 48), :]

    order = (0, 3, 1, 2)
    sent = []
    for t in order:
        x_first = KINDS[t][2]
        u, v = (x, z) if x_first else (z, x)
        pltpu.make_async_copy(shards[t], slot(t, owner), own_sem.at[t]).start()
        for k, d in enumerate(NEAR):
            copy = remote(
                shards[t],
                slot(t, owner),
                send.at[t, k],
                recv.at[t, owner],
                {"fsdp": joined(ring(u, d), v, x_first)},
            )
            copy.start()
            sent.append(copy)

    holds = x == y

    @pl.when(holds)
    def _():
        pltpu.make_async_copy(dense, band(z), own_sem.at[4]).start()
        for k, d in enumerate(NEAR):
            remote(
                dense, band(z), dsend.at[k], drecv.at[z], {"fsdp": ring(x, d) * 4 + z}
            ).start()

    for t in order:
        x_first = KINDS[t][2]
        u, v = (x, z) if x_first else (z, x)
        for d in (0, 1, 3, 2):
            s = joined(ring(u, 4 - d), v, x_first)
            if d:
                remote(shards[t], slot(t, s), send.at[t, 0], recv.at[t, s], sibling).wait_recv()
            for k, e in enumerate(NEAR):
                copy = remote(
                    slot(t, s) if d else shards[t],
                    slot(t, s),
                    send.at[t, 3 + 3 * d + k],
                    recv.at[t, s],
                    {"fsdp": joined(u, ring(v, e), x_first)},
                )
                copy.start()
                sent.append(copy)

    @pl.when(holds)
    def _():
        pltpu.make_async_copy(dense, band(z), own_sem.at[4]).wait()

    @pl.when(jnp.logical_not(holds))
    def _():
        remote(dense, band(z), dsend.at[0], drecv.at[z], sibling).wait_recv()

    dense_sent = []
    for k, e in enumerate(NEAR):
        copy = remote(
            band(z), band(z), dsend.at[3 + k], drecv.at[z], {"fsdp": x * 4 + ring(z, e)}
        )
        copy.start()
        dense_sent.append(copy)

    across = []
    for t in order:
        x_first = KINDS[t][2]
        u, v = (x, z) if x_first else (z, x)
        pltpu.make_async_copy(shards[t], slot(t, owner), own_sem.at[t]).wait()
        for e in NEAR:
            for d in (0, 1, 3, 2):
                s = joined(ring(u, 4 - d), ring(v, 4 - e), x_first)
                remote(shards[t], slot(t, s), send.at[t, 0], recv.at[t, s], sibling).wait_recv()
        copy = remote(wholes[t].at[layer], wholes[t].at[layer], csend.at[t], crecv.at[t], sibling)
        copy.start()
        across.append(copy)
    for e in NEAR:
        i = ring(z, 4 - e)
        remote(dense, band(i), dsend.at[0], drecv.at[i], sibling).wait_recv()
    copy = remote(dense_whole.at[layer], dense_whole.at[layer], csend.at[4], crecv.at[4], sibling)
    copy.start()
    across.append(copy)

    for copy in sent + dense_sent:
        copy.wait_send()

    @pl.when(holds)
    def _():
        for k in range(3):
            remote(dense, band(z), dsend.at[k], drecv.at[z], sibling).wait_send()

    for t, copy in enumerate(across):
        copy.wait_send()
    for t in range(5):
        whole = wholes[t] if t < 4 else dense_whole
        remote(whole.at[layer], whole.at[1 - layer], csend.at[t], crecv.at[t], sibling).wait_recv()


def gather_weights(shards, dense):
    hbm = pl.BlockSpec(memory_space=pl.ANY)
    dma = pltpu.SemaphoreType.DMA
    return pl.pallas_call(
        gather_kernel,
        out_shape=[jax.ShapeDtypeStruct((2, 16 * rows, cols), BF16) for rows, cols, _ in KINDS]
        + [jax.ShapeDtypeStruct((2, GROUP, WIDTH), BF16)],
        in_specs=[hbm] * 5,
        out_specs=[hbm] * 5,
        scratch_shapes=[dma((4, 15)), dma((4, 16)), dma((5,)), dma((6,)), dma((4,)), dma((5,)), dma((5,))],
        compiler_params=pltpu.CompilerParams(collective_id=1, has_side_effects=True),
        name="gather_weights",
    )(*shards, dense)


def turn_tables(tab_ref, odd, sign):
    tables = []
    for i in range(3):
        table = jnp.where(odd, tab_ref[3 + i], tab_ref[i])
        if i and sign < 0:
            table = -table
        tables.append(jnp.concatenate([table] * 3, axis=1))
    return tables


def turn(values, tables):
    cosine, low_sine, high_sine = tables
    span = values.shape[1]
    return (
        values * cosine
        + pltpu.roll(values, span - 8, 1) * low_sine
        + pltpu.roll(values, 8, 1) * high_sine
    )


def column_block(shape):
    col = lax.broadcasted_iota(jnp.int32, shape, 1)
    return lax.shift_right_logical(col * 43691, 21)


def piece_mask(shape):
    row = lax.broadcasted_iota(jnp.int32, shape, 0)
    return lax.shift_right_logical(row, 4) == column_block(shape)


def joint_mask(shape, y):
    row = lax.broadcasted_iota(jnp.int32, shape, 0)
    k = (row & 15) - 7
    chunk = 3 * lax.shift_right_logical(row, 4) + k
    block = column_block(shape)
    wanted = 16 * lax.shift_right_logical(block, 2) + (block & 3) + 4 * y
    return (k >= 0) & (k < 3) & (chunk == wanted)


def spread_matrix():
    shape = (128, WIDTH)
    col = lax.broadcasted_iota(jnp.int32, shape, 1)
    row = lax.broadcasted_iota(jnp.int32, shape, 0)
    return jnp.where(col - 48 * column_block(shape) == row, 1.0, 0.0).astype(BF16)


def layers_kernel(
    x_ref, cot_ref, pos_ref, tab_ref, wq, we, ws, vec, wd,
    lo_out, ig_out, dq_out, de_out, ds_out, dv_out, dd_out,
    xall, dyall, posall, part, psend, prec, qkvs, probs, ctx, acts, slopes,
    n1s, n2s, xhs, vrows, bqs, grows, cur, staged, arrived,
    asend, arecv, rsend, rrecv, posend, porecv, csend, crecv,
):
    micro = lax.axis_index("section")
    y = lax.axis_index("seq")
    sibling = {"section": 1 - micro}
    greet(seq_peers(y) + [sibling])
    own = pl.ds(pl.multiple_of(y * TOK, TOK), TOK)

    def rows_of(i):
        return pl.ds(pl.multiple_of(i * TOK, TOK), TOK)

    def share(ref, sends, recvs):
        copies = []
        for k, d in enumerate(NEAR):
            copy = remote(ref.at[own, :], ref.at[own, :], sends.at[k], recvs.at[k], {"seq": ring(y, d)})
            copy.start()
            copies.append(copy)
        return copies

    def collect(ref, copies, sends, recvs):
        for k, d in enumerate(NEAR):
            src = ref.at[rows_of(ring(y, 4 - d)), :]
            remote(src, src, sends.at[k], recvs.at[k], sibling).wait_recv()
        for copy in copies:
            copy.wait_send()

    def reduce_rows(value, back, l):
        part[...] = value
        psend[back, l] = value.astype(BF16)
        copies = []
        for k, d in enumerate(NEAR):
            to = ring(y, d)
            copy = remote(
                psend.at[back, l, rows_of(to), :],
                prec.at[back, l, k],
                rsend.at[back, l, k],
                rrecv.at[back, l, k],
                {"seq": to},
            )
            copy.start()
            copies.append(copy)
        for copy in copies:
            copy.wait()
        total = part[own, :]
        for k in range(3):
            total = total + prec[back, l, k].astype(F32)
        return total

    posall[own, :] = pos_ref[...]
    pos_copies = share(posall, posend, porecv)

    spread = spread_matrix()
    pieces = piece_mask((LEN, WIDTH))
    joints = joint_mask((LEN, 3 * GROUP), y)
    for l in range(2):
        columns = dot(vec[l], spread)
        vrows[l] = jnp.sum(
            jnp.where(pieces, columns, 0.0).reshape(16, 16, WIDTH), axis=0
        )
        bqs[l] = jnp.broadcast_to(
            jnp.sum(jnp.where(joints, columns[:, : 3 * GROUP], 0.0), axis=0, keepdims=True),
            (8, 3 * GROUP),
        )
    cur[...] = x_ref[...]
    collect(posall, pos_copies, posend, porecv)
    token = lax.broadcasted_iota(jnp.int32, (LEN, 128), 0)
    odd = posall[...] > 2 * token

    def forward(l, carry):
        xall[l, own, :] = cur[...]
        here = xall.at[l]
        collect(here, share(here, asend.at[0, l], arecv.at[0, l]), asend.at[0, l], arecv.at[0, l])
        values = xall[l].astype(F32)
        center = values - jnp.mean(values, axis=-1, keepdims=True)
        scale = lax.rsqrt(jnp.mean(center * center, axis=-1, keepdims=True) + 1e-5)
        normed = center * scale
        xhs[l] = normed
        n1 = (normed * vrows[l, 0:1, :] + vrows[l, 1:2, :]).astype(BF16)
        n2 = (normed * vrows[l, 2:3, :] + vrows[l, 3:4, :]).astype(BF16)
        n1s[l] = n1
        n2s[l] = n2
        joint = dot(n1, wq[l]) + bqs[l, 0:1, :]
        turned = turn(joint[:, : 2 * GROUP], turn_tables(tab_ref, odd, 1))
        qkvs[l, :, : 2 * GROUP] = turned.astype(BF16)
        qkvs[l, :, 2 * GROUP :] = joint[:, 2 * GROUP :].astype(BF16)
        row = lax.broadcasted_iota(jnp.int32, (LEN, LEN), 0)
        allowed = row >= lax.broadcasted_iota(jnp.int32, (LEN, LEN), 1)
        for n in range(3):
            q = qkvs[l, :, n * HD : (n + 1) * HD]
            k = qkvs[l, :, GROUP + n * HD : GROUP + (n + 1) * HD]
            v = qkvs[l, :, 2 * GROUP + n * HD : 2 * GROUP + (n + 1) * HD]
            scores = jnp.where(allowed, dot_nt(q, k) * HD**-0.5, -1e30)
            powers = jnp.exp(scores - jnp.max(scores, axis=-1, keepdims=True))
            prob = powers / jnp.sum(powers, axis=-1, keepdims=True)
            probs[l, n] = prob
            ctx[l, :, n * HD : (n + 1) * HD] = dot(prob.astype(BF16), v).astype(BF16)
        hidden = dot(n2, we[l]) + vrows[l, 6:7, :]
        phi = 0.5 + 0.5 * lax.erf(hidden * math.sqrt(0.5))
        acts[l] = (hidden * phi).astype(BF16)
        density = jnp.exp(-0.5 * hidden * hidden) * (1.0 / math.sqrt(2.0 * math.pi))
        slopes[l] = phi + hidden * density
        total = reduce_rows(dot(ctx[l], wd[l]) + dot(acts[l], ws[l]), 0, l)
        result = cur[...].astype(F32) + total + vrows[l, 4:5, :] + vrows[l, 5:6, :]
        cur[...] = result.astype(BF16)
        staged[0, l] = cur[...]
        return carry

    lax.fori_loop(0, 2, forward, 0)
    lo_copy = remote(staged.at[0, 1 - micro], arrived.at[0], csend.at[0], crecv.at[0], sibling)
    lo_copy.start()
    cur[...] = cot_ref[...]

    def backward(i, carry):
        l = 1 - i
        dyall[l, own, :] = cur[...]
        here = dyall.at[l]
        collect(here, share(here, asend.at[1, l], arecv.at[1, l]), asend.at[1, l], arecv.at[1, l])
        out_grad = dyall[l]
        hidden_grad = (dot_nt(out_grad, ws[l]) * slopes[l]).astype(BF16)
        ds_out[l] = dot_tn(acts[l], out_grad).astype(BF16)
        de_out[l] = dot_tn(n2s[l], hidden_grad).astype(BF16)
        n2_grad = dot_nt(hidden_grad, we[l])
        ctx_grad = dot_nt(out_grad, wd[l]).astype(BF16)
        dd_out[l] = dot_tn(ctx[l], out_grad).astype(BF16)
        parts = ([], [], [])
        for n in range(3):
            q = qkvs[l, :, n * HD : (n + 1) * HD]
            k = qkvs[l, :, GROUP + n * HD : GROUP + (n + 1) * HD]
            v = qkvs[l, :, 2 * GROUP + n * HD : 2 * GROUP + (n + 1) * HD]
            up = ctx_grad[:, n * HD : (n + 1) * HD]
            prob = probs[l, n]
            prob_grad = dot_nt(up, v)
            inner = jnp.sum(prob * prob_grad, axis=-1, keepdims=True)
            score_grad = (prob * (prob_grad - inner)).astype(BF16)
            parts[0].append(dot(score_grad, k) * HD**-0.5)
            parts[1].append(dot_tn(score_grad, q) * HD**-0.5)
            parts[2].append(dot_tn(prob.astype(BF16), up))
        turned_grad = jnp.concatenate(parts[0] + parts[1], axis=1).astype(BF16).astype(F32)
        joint_grad = jnp.concatenate(
            [turn(turned_grad, turn_tables(tab_ref, odd, -1))] + parts[2], axis=1
        ).astype(BF16)
        dq_out[l] = dot_tn(n1s[l], joint_grad).astype(BF16)
        n1_grad = dot_nt(joint_grad, wq[l])
        normed = xhs[l]
        grows[...] = jnp.zeros_like(grows)
        grows[0:1, :] = jnp.sum(n1_grad * normed, axis=0, keepdims=True)
        grows[1:2, :] = jnp.sum(n1_grad, axis=0, keepdims=True)
        grows[2:3, :] = jnp.sum(n2_grad * normed, axis=0, keepdims=True)
        grows[3:4, :] = jnp.sum(n2_grad, axis=0, keepdims=True)
        grows[4:5, :] = jnp.sum(cur[...].astype(F32), axis=0, keepdims=True)
        grows[6:7, :] = jnp.sum(hidden_grad.astype(F32), axis=0, keepdims=True)
        joint_bias = jnp.sum(joint_grad.astype(F32), axis=0, keepdims=True)
        spread_now = spread_matrix()
        first = jnp.where(piece_mask((LEN, WIDTH)), jnp.concatenate([grows[...]] * 16, axis=0), 0.0)
        second = jnp.where(
            joint_mask((LEN, 3 * GROUP), y), jnp.broadcast_to(joint_bias, (LEN, 3 * GROUP)), 0.0
        )
        dv_out[l] = (
            dot_nt(first.astype(BF16), spread_now)
            + dot_nt(second.astype(BF16), spread_now[:, : 3 * GROUP])
        ).astype(BF16)
        total = reduce_rows(n1_grad * vrows[l, 0:1, :] + n2_grad * vrows[l, 2:3, :], 1, l)
        values = xall[l, own, :].astype(F32)
        center = values - jnp.mean(values, axis=-1, keepdims=True)
        scale = lax.rsqrt(jnp.mean(center * center, axis=-1, keepdims=True) + 1e-5)
        near = center * scale
        pulled = scale * (
            total
            - jnp.mean(total, axis=-1, keepdims=True)
            - near * jnp.mean(total * near, axis=-1, keepdims=True)
        )
        cur[...] = (cur[...].astype(F32) + pulled).astype(BF16)
        staged[1, l] = cur[...]
        return carry

    lax.fori_loop(0, 2, backward, 0)
    ig_copy = remote(staged.at[1, 1 - micro], arrived.at[1], csend.at[1], crecv.at[1], sibling)
    ig_copy.start()
    lo_copy.wait()
    ig_copy.wait()
    lo_out[micro] = staged[0, micro]
    lo_out[1 - micro] = arrived[0]
    ig_out[micro] = staged[1, micro]
    ig_out[1 - micro] = arrived[1]


def run_layers(tokens, cot, spots, tables, wholes, dense_whole):
    vmem = pl.BlockSpec(memory_space=pltpu.VMEM)
    dma = pltpu.SemaphoreType.DMA
    shapes = (
        [(2, TOK, WIDTH), (2, TOK, WIDTH)]
        + [(2, 16 * rows, cols) for rows, cols, _ in KINDS]
        + [(2, GROUP, WIDTH)]
    )
    return pl.pallas_call(
        layers_kernel,
        out_shape=[jax.ShapeDtypeStruct(shape, BF16) for shape in shapes],
        in_specs=[vmem] * 9,
        out_specs=[vmem] * 7,
        scratch_shapes=[
            pltpu.VMEM((2, LEN, WIDTH), BF16),
            pltpu.VMEM((2, LEN, WIDTH), BF16),
            pltpu.VMEM((LEN, 128), jnp.int32),
            pltpu.VMEM((LEN, WIDTH), F32),
            pltpu.VMEM((2, 2, LEN, WIDTH), BF16),
            pltpu.VMEM((2, 2, 3, TOK, WIDTH), BF16),
            pltpu.VMEM((2, LEN, 3 * GROUP), BF16),
            pltpu.VMEM((2, 3, LEN, LEN), F32),
            pltpu.VMEM((2, LEN, GROUP), BF16),
            pltpu.VMEM((2, LEN, WIDTH), BF16),
            pltpu.VMEM((2, LEN, WIDTH), F32),
            pltpu.VMEM((2, LEN, WIDTH), BF16),
            pltpu.VMEM((2, LEN, WIDTH), BF16),
            pltpu.VMEM((2, LEN, WIDTH), F32),
            pltpu.VMEM((2, 16, WIDTH), F32),
            pltpu.VMEM((2, 8, 3 * GROUP), F32),
            pltpu.VMEM((16, WIDTH), F32),
            pltpu.VMEM((TOK, WIDTH), BF16),
            pltpu.VMEM((2, 2, TOK, WIDTH), BF16),
            pltpu.VMEM((2, TOK, WIDTH), BF16),
            dma((2, 2, 3)),
            dma((2, 2, 3)),
            dma((2, 2, 3)),
            dma((2, 2, 3)),
            dma((3,)),
            dma((3,)),
            dma((2,)),
            dma((2,)),
        ],
        compiler_params=pltpu.CompilerParams(
            collective_id=2, has_side_effects=True, vmem_limit_bytes=60 * MIB
        ),
        name="layers",
    )(tokens, cot, spots, tables, *wholes, dense_whole)


def reduce_kernel(*refs):
    grads, dense_grad = refs[0:4], refs[4]
    outs, dense_out = refs[5:9], refs[9]
    accs, dense_acc = refs[10:14], refs[14]
    sibs, dense_sib = refs[15:19], refs[19]
    wides, dense_wide = refs[20:24], refs[24]
    mids = refs[25:29]
    narrows, dense_narrow = refs[29:33], refs[33]
    ends, dense_end = refs[34:38], refs[38]
    own_sem, csend, crecv, asend, arecv, bsend, brecv, ysend, yrecv = refs[39:]
    layer = lax.axis_index("section")
    y = lax.axis_index("seq")
    owner, x, z = places()
    sibling = {"section": 1 - layer}
    greet(sheet_peers(x, z) + seq_peers(y) + [sibling])
    holds = x == y

    all_grads = list(grads) + [dense_grad]
    all_accs = list(accs) + [dense_acc]
    all_sibs = list(sibs) + [dense_sib]
    order = (2, 1, 4, 0, 3)
    own_copies, sib_copies = {}, {}
    for t in order:
        own_copies[t] = pltpu.make_async_copy(all_grads[t].at[layer], all_accs[t], own_sem.at[t])
        own_copies[t].start()
        sib_copies[t] = remote(
            all_grads[t].at[1 - layer], all_sibs[t], csend.at[t], crecv.at[t], sibling
        )
        sib_copies[t].start()

    sent = []
    for t in order:
        own_copies[t].wait()
        sib_copies[t].wait_recv()
        if t == 4:
            for i in range(4):
                dense_acc[i] = (dense_acc[i].astype(F32) + dense_sib[i].astype(F32)).astype(BF16)
            for k, e in enumerate(NEAR):
                to = ring(z, e)
                copy = remote(
                    dense_acc.at[to], dense_wide.at[k], asend.at[t, k], arecv.at[t, k], {"fsdp": x * 4 + to}
                )
                copy.start()
                sent.append(copy)
            continue
        acc, sib = accs[t], sibs[t]

        def add(i, carry, acc=acc, sib=sib):
            a, b = lax.div(i, 4), lax.rem(i, 4)
            acc[a, b] = (acc[a, b].astype(F32) + sib[a, b].astype(F32)).astype(BF16)
            return carry

        lax.fori_loop(0, 16, add, 0)
        x_first = KINDS[t][2]
        u, v = (x, z) if x_first else (z, x)
        for k, e in enumerate(NEAR):
            to = ring(v, e)
            copy = remote(
                acc.at[:, to] if x_first else acc.at[to],
                wides[t].at[k],
                asend.at[t, k],
                arecv.at[t, k],
                {"fsdp": joined(u, to, x_first)},
            )
            copy.start()
            sent.append(copy)

    last = {}
    for t in order:
        if t == 4:
            for k in range(3):
                remote(dense_acc.at[0], dense_wide.at[k], asend.at[t, k], arecv.at[t, k], sibling).wait_recv()
            total = dense_acc[z].astype(F32)
            for k in range(3):
                total = total + dense_wide[k].astype(F32)
            dense_end[...] = total.astype(BF16)

            @pl.when(jnp.logical_not(holds))
            def _():
                away = lax.rem(x - y + 4, 4)
                remote(
                    dense_end, dense_narrow.at[away - 1], bsend.at[4, 0], brecv.at[4, away - 1], {"fsdp": y * 4 + z}
                ).start()

            continue
        acc = accs[t]
        x_first = KINDS[t][2]
        u, v = (x, z) if x_first else (z, x)
        for k in range(3):
            remote(wides[t].at[k], wides[t].at[k], asend.at[t, k], arecv.at[t, k], sibling).wait_recv()
        for d in (1, 3, 2, 0):
            to = ring(u, d)
            total = acc[to, v].astype(F32) if x_first else acc[v, to].astype(F32)
            for k in range(3):
                total = total + wides[t][k, to].astype(F32)
            if d == 0:
                last[t] = None
            mids[t][to] = total.astype(BF16)
            if d:
                k = NEAR.index(d)
                copy = remote(
                    mids[t].at[to],
                    narrows[t].at[k],
                    bsend.at[t, k],
                    brecv.at[t, k],
                    {"fsdp": joined(to, v, x_first)},
                )
                copy.start()
                sent.append(copy)

    for t in order:
        if t == 4:

            @pl.when(holds)
            def _():
                for k in range(3):
                    remote(dense_end, dense_narrow.at[k], bsend.at[4, 0], brecv.at[4, k], sibling).wait_recv()
                total = dense_end[...].astype(F32)
                for k in range(3):
                    total = total + dense_narrow[k].astype(F32)
                dense_out[...] = total.astype(BF16)
                for k, d in enumerate(NEAR):
                    remote(dense_out, dense_out, ysend.at[4, k], yrecv.at[4, 0], {"seq": ring(y, d)}).start()

            continue
        x_first = KINDS[t][2]
        u, v = (x, z) if x_first else (z, x)
        for k in range(3):
            remote(narrows[t].at[k], narrows[t].at[k], bsend.at[t, k], brecv.at[t, k], sibling).wait_recv()
        total = mids[t][u].astype(F32)
        for k in range(3):
            total = total + narrows[t][k].astype(F32)
        ends[t][y] = total.astype(BF16)
        for k, d in enumerate(NEAR):
            copy = remote(
                ends[t].at[y], ends[t].at[y], ysend.at[t, k], yrecv.at[t, k], {"seq": ring(y, d)}
            )
            copy.start()
            sent.append(copy)

    for t in range(4):
        for k, d in enumerate(NEAR):
            src = ends[t].at[ring(y, 4 - d)]
            remote(src, src, ysend.at[t, k], yrecv.at[t, k], sibling).wait_recv()
        outs[t][...] = ends[t][...]

    @pl.when(holds)
    def _():
        for k in range(3):
            remote(dense_out, dense_out, ysend.at[4, k], yrecv.at[4, 0], sibling).wait_send()

    @pl.when(jnp.logical_not(holds))
    def _():
        remote(dense_out, dense_out, ysend.at[4, 0], yrecv.at[4, 0], sibling).wait_recv()
        remote(dense_end, dense_narrow.at[0], bsend.at[4, 0], brecv.at[4, 0], sibling).wait_send()

    for copy in sent:
        copy.wait_send()
    for t in order:
        sib_copies[t].wait_send()


def reduce_grads(grads, dense_grad):
    hbm = pl.BlockSpec(memory_space=pl.ANY)
    vmem = pl.BlockSpec(memory_space=pltpu.VMEM)
    dma = pltpu.SemaphoreType.DMA
    sizes = [(rows, cols) for rows, cols, _ in KINDS]

    def each(*lead):
        return [pltpu.VMEM((*lead, rows, cols), BF16) for rows, cols in sizes]

    def dense(*lead):
        return [pltpu.VMEM((*lead, 48, WIDTH), BF16)]

    return pl.pallas_call(
        reduce_kernel,
        out_shape=[jax.ShapeDtypeStruct((4, rows, cols), BF16) for rows, cols in sizes]
        + [jax.ShapeDtypeStruct((48, WIDTH), BF16)],
        in_specs=[hbm] * 5,
        out_specs=[vmem] * 5,
        scratch_shapes=each(4, 4)
        + dense(4)
        + each(4, 4)
        + dense(4)
        + each(3, 4)
        + dense(3)
        + each(4)
        + each(3)
        + dense(3)
        + each(4)
        + dense()
        + [dma((5,)), dma((5,)), dma((5,)), dma((5, 3)), dma((5, 3)), dma((5, 3)), dma((5, 3)), dma((5, 3)), dma((5, 3))],
        compiler_params=pltpu.CompilerParams(
            collective_id=3, has_side_effects=True, vmem_limit_bytes=60 * MIB
        ),
        name="reduce_grads",
    )(*grads, dense_grad)


def angle_tables():
    lane = np.arange(128) % HD
    frequency = np.exp(-math.log(10000.0) * (2.0 / ROT) * np.arange(ROT // 2)).astype(np.float32)
    tables = []
    for offset in (0, 1):
        spots = (2 * np.arange(LEN) + offset).astype(np.float32)
        angle = (spots[:, None] * frequency[None, :])[:, lane % 8].astype(np.float64)
        cosine = np.where(lane < ROT, np.cos(angle), 1.0)
        low_sine = np.where(lane < 8, -np.sin(angle), 0.0)
        high_sine = np.where((lane >= 8) & (lane < ROT), np.sin(angle), 0.0)
        tables += [cosine, low_sine, high_sine]
    return np.stack(tables).astype(np.float32)


def on_device(
    tokens_in, cotangent, positions, first_gain, first_bias, second_gain, second_bias,
    qkv_weight, qkv_bias, dense_weight, dense_bias, expand_weight, expand_bias,
    shrink_weight, shrink_bias,
):
    micro = lax.axis_index("section")
    y = lax.axis_index("seq")
    tokens = lax.dynamic_index_in_dim(tokens_in, micro, 0, keepdims=False)[0]
    cot = lax.dynamic_index_in_dim(cotangent, micro, 0, keepdims=False)[0]
    spots = lax.dynamic_index_in_dim(positions, micro, 0, keepdims=False)[0]
    spots = jnp.broadcast_to(spots[:, None], (TOK, 128))

    joint = lax.dynamic_index_in_dim(qkv_weight.reshape(48, 3, 4, GROUP), y, 2, keepdims=False)
    joint = joint.reshape(48, 3 * GROUP)
    expand = lax.dynamic_index_in_dim(expand_weight.reshape(48, 16, 4, 48), y, 2, keepdims=False)
    expand = expand.reshape(48, WIDTH)
    shrink = lax.dynamic_slice(shrink_weight[0], (48 * y, 0), (48, WIDTH))
    hidden_bias = lax.dynamic_slice(expand_bias, (0, 48 * y), (1, 48))
    vector = jnp.concatenate(
        [first_gain, first_bias, second_gain, second_bias, dense_bias, shrink_bias, hidden_bias]
        + [qkv_bias.reshape(3, 48), jnp.zeros((6, 48), BF16)],
        axis=0,
    )
    vector = jnp.pad(vector, ((0, 0), (0, 80)))

    *wholes, dense_whole = gather_weights((joint, expand, shrink, vector), dense_weight[0])
    layer_out, input_grad, *grads = run_layers(
        tokens, cot, spots, jnp.asarray(angle_tables()), wholes, dense_whole
    )
    shaped = [
        grad.reshape(2, 4, 4, rows, cols) for grad, (rows, cols, _) in zip(grads[:4], KINDS)
    ]
    joint, expand, shrink, vector, dense = reduce_grads(shaped, grads[4].reshape(2, 4, 48, WIDTH))

    joint = joint.reshape(4, 48, 3, GROUP).transpose(1, 2, 0, 3).reshape(1, 48, 3 * WIDTH)
    expand = expand.reshape(4, 48, 16, 48).transpose(1, 2, 0, 3).reshape(1, 48, 4 * WIDTH)
    shrink = shrink.reshape(1, GROUP, WIDTH)
    vector = vector[:, :, :48].astype(F32)
    summed = jnp.sum(vector, axis=0)
    hidden_bias = vector[:, 6].reshape(1, GROUP)
    shape = (1, 2, 1, TOK, WIDTH)
    return (
        layer_out.reshape(shape),
        input_grad.reshape(shape),
        summed[0:1],
        summed[1:2],
        summed[2:3],
        summed[3:4],
        joint.astype(F32),
        summed[7:10].reshape(1, 144),
        dense[None].astype(F32),
        summed[4:5],
        expand.astype(F32),
        hidden_bias,
        shrink.astype(F32),
        summed[4:5],
    )


def solution(mesh):
    tokens = P(None, "fsdp", "seq", None)
    flat = P("section", "fsdp")
    wide = P("section", "fsdp", None)
    out = P("section", None, "fsdp", "seq", None)
    return jax.shard_map(
        on_device,
        mesh=mesh,
        in_specs=(
            tokens, tokens, P(None, "fsdp", "seq"), flat, flat, flat, flat,
            wide, flat, wide, flat, wide, flat, wide, flat,
        ),
        out_specs=(
            out, out, flat, flat, flat, flat, wide, flat, wide, flat, wide, flat, wide, flat,
        ),
        check_vma=False,
    )
```

```python
import math

import jax
import jax.numpy as jnp
import numpy as np
from jax import lax
from jax.experimental import pallas as pl
from jax.experimental.pallas import tpu as pltpu
from jax.sharding import PartitionSpec as P

MESH = pl.DeviceIdType.MESH
F32 = jnp.float32
BF16 = jnp.bfloat16
HD = 64
ROT = 16
WIDTH = 768
TOK = 64
LEN = 256
GROUP = 192
NEAR = (1, 3, 2)
MIB = 1024 * 1024

KINDS = ((48, 576, False), (48, 768, True), (48, 768, False), (16, 128, True))


def ring(value, by):
    return lax.rem(value + by, 4)


def places():
    owner = lax.axis_index("fsdp")
    return owner, lax.div(owner, 4), lax.rem(owner, 4)


def joined(u, v, x_first):
    return u * 4 + v if x_first else v * 4 + u


def remote(src, dst, send, recv, target):
    return pltpu.make_async_remote_copy(
        src_ref=src, dst_ref=dst, send_sem=send, recv_sem=recv, device_id=target, device_id_type=MESH
    )


def greet(targets):
    barrier = pltpu.get_barrier_semaphore()
    for target in targets:
        pl.semaphore_signal(barrier, inc=1, device_id=target, device_id_type=MESH)
    pl.semaphore_wait(barrier, len(targets))


def sheet_peers(x, z):
    return [{"fsdp": ring(x, d) * 4 + z} for d in (1, 2, 3)] + [
        {"fsdp": x * 4 + ring(z, d)} for d in (1, 2, 3)
    ]


def seq_peers(y):
    return [{"seq": ring(y, d)} for d in (1, 2, 3)]


def dot(a, b):
    return jnp.dot(a, b, preferred_element_type=F32)


def dot_nt(a, b):
    return lax.dot_general(a, b, (((1,), (1,)), ((), ())), preferred_element_type=F32)


def dot_tn(a, b):
    return lax.dot_general(a, b, (((0,), (0,)), ((), ())), preferred_element_type=F32)


def turn_tables(tab_ref, odd, sign):
    tables = []
    for i in range(3):
        table = jnp.where(odd, tab_ref[3 + i], tab_ref[i])
        if i and sign < 0:
            table = -table
        tables.append(jnp.concatenate([table] * 3, axis=1))
    return tables


def turn(values, tables):
    cosine, low_sine, high_sine = tables
    span = values.shape[1]
    return (
        values * cosine
        + pltpu.roll(values, span - 8, 1) * low_sine
        + pltpu.roll(values, 8, 1) * high_sine
    )


def column_block(shape):
    col = lax.broadcasted_iota(jnp.int32, shape, 1)
    return lax.shift_right_logical(col * 43691, 21)


def piece_mask(shape):
    row = lax.broadcasted_iota(jnp.int32, shape, 0)
    return lax.shift_right_logical(row, 4) == column_block(shape)


def joint_mask(shape, y):
    row = lax.broadcasted_iota(jnp.int32, shape, 0)
    k = (row & 15) - 7
    chunk = 3 * lax.shift_right_logical(row, 4) + k
    block = column_block(shape)
    wanted = 16 * lax.shift_right_logical(block, 2) + (block & 3) + 4 * y
    return (k >= 0) & (k < 3) & (chunk == wanted)


def spread_matrix():
    shape = (128, WIDTH)
    col = lax.broadcasted_iota(jnp.int32, shape, 1)
    row = lax.broadcasted_iota(jnp.int32, shape, 0)
    return jnp.where(col - 48 * column_block(shape) == row, 1.0, 0.0).astype(BF16)

ORDER = (0, 3, 1, 2)
BACK = (2, 1, 4, 0, 3)


def program_kernel(*refs):
    (
        x_ref, cot_ref, pos_ref, tab_ref, fg, fb, sg, sb, db, hb, qb, eb, qw, ew, sw, dw,
        out_q, out_e, out_s, out_v, out_d, lo_out, ig_out,
        qs, es, vs, vecf, wq, we, ws, wv, wd,
        dq, de, ds, dv, dd, hq, he, hs, hv, hd, aq, ae, as_, av, ad,
        mq, me, ms, mv, md, nq, ne, ns, nv, nd,
        xall, dyall, posall, part, psend, prec, qkvs, probs, ctx, acts, slopes,
        n1s, n2s, xhs, vrows, bqs, grows, staged,
        gsend, grecv, dsend, drecv, csend, crecv,
        asend, arecv, rsend, rrecv, posend, porecv,
        hsend, hrecv, wsend, wrecv, bsend, brecv, ysend, yrecv, osend, orecv,
    ) = refs
    micro = lax.axis_index("section")
    y = lax.axis_index("seq")
    owner, x, z = places()
    sibling = {"section": 1 - micro}
    holds = x == y
    own = pl.ds(pl.multiple_of(y * TOK, TOK), TOK)

    peers = sheet_peers(x, z) + seq_peers(y) + [sibling]
    barrier = pltpu.get_barrier_semaphore()
    for target in peers:
        pl.semaphore_signal(barrier, inc=1, device_id=target, device_id_type=MESH)

    vecf[...] = jnp.zeros_like(vecf)
    for i, ref in enumerate((fg, fb, sg, sb, db, hb)):
        vecf[i : i + 1, 0:48] = ref[...].astype(F32)
    for k in range(3):
        vecf[7 + k : 8 + k, 0:48] = qb[:, 48 * k : 48 * k + 48].astype(F32)
    for h in range(4):

        @pl.when(y == h)
        def _():
            qs[...] = jnp.concatenate(
                [qw[0, :, WIDTH * t + GROUP * h : WIDTH * t + GROUP * (h + 1)] for t in range(3)], axis=1
            )
            es[...] = jnp.concatenate(
                [ew[0, :, GROUP * f + 48 * h : GROUP * f + 48 * h + 48] for f in range(16)], axis=1
            )
            vecf[6:7, 0:48] = eb[:, 48 * h : 48 * h + 48].astype(F32)

    vs[...] = vecf[...].astype(BF16)
    shrink_rows = sw.at[0, pl.ds(pl.multiple_of(48 * y, 16), 48), :]
    shards = (qs, es, shrink_rows, vs)
    wholes = (wq, we, ws, wv, wd)

    def slot(t, l, s):
        rows = KINDS[t][0]
        return wholes[t].at[l, pl.ds(pl.multiple_of(s * rows, 16), rows), :]

    def band(l, i):
        return wd.at[l, pl.ds(pl.multiple_of(i * 48, 16), 48), :]

    def mine(rows):
        return pl.ds(pl.multiple_of(owner * rows, 16), rows)

    wq[micro, mine(48), :] = qs[...]
    we[micro, mine(48), :] = es[...]
    ws[micro, mine(48), :] = shrink_rows[...]
    wv[micro, mine(16), :] = vs[...]
    dense_mine = pl.ds(pl.multiple_of(z * 48, 16), 48)

    @pl.when(holds)
    def _():
        wd[micro, dense_mine, :] = dw[0]

    xall[0, own, :] = x_ref[micro, 0]
    dyall[1, own, :] = cot_ref[micro, 0]
    shape = (TOK, TOK)
    level = lax.broadcasted_iota(jnp.int32, shape, 0) == lax.broadcasted_iota(jnp.int32, shape, 1)
    spots = jnp.where(level, jnp.broadcast_to(pos_ref[micro].astype(F32), shape), 0.0)
    posall[own, :] = jnp.broadcast_to(jnp.sum(spots, axis=1, keepdims=True), (TOK, 128))
    pl.semaphore_wait(barrier, len(peers))

    def axes(t):
        x_first = KINDS[t][2]
        return (x, z, x_first) if x_first else (z, x, x_first)

    def gather_start(l):
        for t in ORDER:
            u, v, x_first = axes(t)
            for k, d in enumerate(NEAR):
                remote(
                    shards[t], slot(t, l, owner), gsend.at[t, k], grecv.at[t, owner],
                    {"fsdp": joined(ring(u, d), v, x_first)},
                ).start()

        @pl.when(holds)
        def _():
            for k, d in enumerate(NEAR):
                remote(
                    dw.at[0], band(l, z), dsend.at[k], drecv.at[z], {"fsdp": ring(x, d) * 4 + z}
                ).start()

    def gather_forward(l):
        for t in ORDER:
            u, v, x_first = axes(t)
            for d in (0, 1, 3, 2):
                s = joined(ring(u, 4 - d), v, x_first)
                if d:
                    remote(slot(t, l, s), slot(t, l, s), gsend.at[t, 0], grecv.at[t, s], sibling).wait_recv()
                for k, e in enumerate(NEAR):
                    remote(
                        slot(t, l, s), slot(t, l, s), gsend.at[t, 3 + 3 * d + k], grecv.at[t, s],
                        {"fsdp": joined(u, ring(v, e), x_first)},
                    ).start()

        @pl.when(jnp.logical_not(holds))
        def _():
            remote(band(l, z), band(l, z), dsend.at[0], drecv.at[z], sibling).wait_recv()

        for k, e in enumerate(NEAR):
            remote(
                band(l, z), band(l, z), dsend.at[3 + k], drecv.at[z], {"fsdp": x * 4 + ring(z, e)}
            ).start()

    def need(t, l):
        @pl.when(micro == l)
        def _():
            if t < 4:
                u, v, x_first = axes(t)
                for e in NEAR:
                    for d in (0, 1, 3, 2):
                        s = joined(ring(u, 4 - d), ring(v, 4 - e), x_first)
                        remote(slot(t, l, s), slot(t, l, s), gsend.at[t, 0], grecv.at[t, s], sibling).wait_recv()
            else:
                for e in NEAR:
                    i = ring(z, 4 - e)
                    remote(band(l, i), band(l, i), dsend.at[0], drecv.at[i], sibling).wait_recv()
            remote(wholes[t].at[l], wholes[t].at[l], csend.at[t], crecv.at[t], sibling).start()

        @pl.when(micro != l)
        def _():
            remote(wholes[t].at[l], wholes[t].at[l], csend.at[t], crecv.at[t], sibling).wait_recv()

    def rows_of(i):
        return pl.ds(pl.multiple_of(i * TOK, TOK), TOK)

    def share(ref, sends, recvs):
        for k, d in enumerate(NEAR):
            remote(ref.at[own, :], ref.at[own, :], sends.at[k], recvs.at[k], {"seq": ring(y, d)}).start()

    def collect(ref, sends, recvs):
        for k, d in enumerate(NEAR):
            src = ref.at[rows_of(ring(y, 4 - d)), :]
            remote(src, src, sends.at[k], recvs.at[k], sibling).wait_recv()

    def reduce_start(value, back, l):
        part[back, l] = value
        psend[back, l] = value.astype(BF16)
        for k, d in enumerate(NEAR):
            to = ring(y, d)
            remote(
                psend.at[back, l, rows_of(to), :], prec.at[back, l, k],
                rsend.at[back, l, k], rrecv.at[back, l, k], {"seq": to},
            ).start()

    def reduce_end(back, l):
        total = part[back, l, own, :]
        for k in range(3):
            remote(
                prec.at[back, l, k], prec.at[back, l, k],
                rsend.at[back, l, k], rrecv.at[back, l, k], sibling,
            ).wait_recv()
            total = total + prec[back, l, k].astype(F32)
        return total

    share(xall.at[0], asend.at[0, 0], arecv.at[0, 0])
    share(posall, posend, porecv)

    @pl.when(micro == 0)
    def _():
        gather_start(0)

    share(dyall.at[1], asend.at[1, 1], arecv.at[1, 1])

    @pl.when(micro == 0)
    def _():
        gather_forward(0)

    collect(posall, posend, porecv)
    token = lax.broadcasted_iota(jnp.int32, (LEN, 128), 0)
    odd = posall[...] > (2 * token).astype(F32) + 0.5

    def forward(l):
        need(3, l)
        columns = dot(wv[l], spread_matrix())
        vrows[l] = jnp.sum(
            jnp.where(piece_mask((LEN, WIDTH)), columns, 0.0).reshape(16, 16, WIDTH), axis=0
        )
        bqs[l] = jnp.broadcast_to(
            jnp.sum(
                jnp.where(joint_mask((LEN, 3 * GROUP), y), columns[:, : 3 * GROUP], 0.0),
                axis=0,
                keepdims=True,
            ),
            (8, 3 * GROUP),
        )
        collect(xall.at[l], asend.at[0, l], arecv.at[0, l])
        values = xall[l].astype(F32)
        center = values - jnp.mean(values, axis=-1, keepdims=True)
        scale = lax.rsqrt(jnp.mean(center * center, axis=-1, keepdims=True) + 1e-5)
        normed = center * scale
        xhs[l] = normed
        n1 = (normed * vrows[l, 0:1, :] + vrows[l, 1:2, :]).astype(BF16)
        n2 = (normed * vrows[l, 2:3, :] + vrows[l, 3:4, :]).astype(BF16)
        n1s[l] = n1
        n2s[l] = n2
        need(0, l)
        joint = dot(n1, wq[l]) + bqs[l, 0:1, :]
        turned = turn(joint[:, : 2 * GROUP], turn_tables(tab_ref, odd, 1))
        qkvs[l, :, : 2 * GROUP] = turned.astype(BF16)
        qkvs[l, :, 2 * GROUP :] = joint[:, 2 * GROUP :].astype(BF16)
        row = lax.broadcasted_iota(jnp.int32, (LEN, LEN), 0)
        allowed = row >= lax.broadcasted_iota(jnp.int32, (LEN, LEN), 1)
        for n in range(3):
            q = qkvs[l, :, n * HD : (n + 1) * HD]
            k = qkvs[l, :, GROUP + n * HD : GROUP + (n + 1) * HD]
            v = qkvs[l, :, 2 * GROUP + n * HD : 2 * GROUP + (n + 1) * HD]
            scores = jnp.where(allowed, dot_nt(q, k) * HD**-0.5, -1e30)
            powers = jnp.exp(scores - jnp.max(scores, axis=-1, keepdims=True))
            prob = powers / jnp.sum(powers, axis=-1, keepdims=True)
            probs[l, n] = prob
            ctx[l, :, n * HD : (n + 1) * HD] = dot(prob.astype(BF16), v).astype(BF16)
        if l == 0:

            @pl.when(micro == 1)
            def _():
                gather_start(1)

        need(1, l)
        hidden = dot(n2, we[l]) + vrows[l, 6:7, :]
        phi = 0.5 + 0.5 * lax.erf(hidden * math.sqrt(0.5))
        acts[l] = (hidden * phi).astype(BF16)
        if l == 0:

            @pl.when(micro == 1)
            def _():
                gather_forward(1)

        need(4, l)
        need(2, l)
        reduce_start(dot(ctx[l], wd[l]) + dot(acts[l], ws[l]), 0, l)
        density = jnp.exp(-0.5 * hidden * hidden) * (1.0 / math.sqrt(2.0 * math.pi))
        slopes[l] = phi + hidden * density

    def forward_end(l):
        total = reduce_end(0, l)
        result = xall[l, own, :].astype(F32) + total + vrows[l, 4:5, :] + vrows[l, 5:6, :]
        return result.astype(BF16)

    grads = (dq, de, ds, dv, dd)
    helds = (hq, he, hs, hv, hd)
    wides = (aq, ae, as_, av, ad)
    mids = (mq, me, ms, mv, md)
    narrows = (nq, ne, ns, nv, nd)
    outs = (out_q, out_e, out_s, out_v, out_d)

    def keep(t, l, value):
        rows = KINDS[t][0] if t < 4 else 48
        value = value.astype(BF16)
        for b in range(value.shape[0] // rows):
            piece = value[b * rows : (b + 1) * rows]
            if t < 4:
                grads[t][l, b // 4, b % 4] = piece
            else:
                grads[t][l, b] = piece

        @pl.when(micro != l)
        def _():
            remote(grads[t].at[l], helds[t], hsend.at[t], hrecv.at[t], sibling).start()

    def fold(t, l):
        remote(helds[t], helds[t], hsend.at[t], hrecv.at[t], sibling).wait_recv()
        grad, held = grads[t], helds[t]
        if t == 4:
            for i in range(4):
                grad[l, i] = (grad[l, i].astype(F32) + held[i].astype(F32)).astype(BF16)
            for k, e in enumerate(NEAR):
                to = ring(z, e)
                remote(
                    grad.at[l, to], wides[t].at[k], wsend.at[t, k], wrecv.at[t, k], {"fsdp": x * 4 + to}
                ).start()
            return

        def add(i, carry):
            a, b = lax.div(i, 4), lax.rem(i, 4)
            grad[l, a, b] = (grad[l, a, b].astype(F32) + held[a, b].astype(F32)).astype(BF16)
            return carry

        lax.fori_loop(0, 16, add, 0)
        u, v, x_first = axes(t)
        for k, e in enumerate(NEAR):
            to = ring(v, e)
            remote(
                grad.at[l, :, to] if x_first else grad.at[l, to],
                wides[t].at[k], wsend.at[t, k], wrecv.at[t, k], {"fsdp": joined(u, to, x_first)},
            ).start()

    def wide_end(t, l):
        grad = grads[t]
        for k in range(3):
            remote(wides[t].at[k], wides[t].at[k], wsend.at[t, k], wrecv.at[t, k], sibling).wait_recv()
        if t == 4:
            total = grad[l, z].astype(F32)
            for k in range(3):
                total = total + wides[t][k].astype(F32)
            mids[t][...] = total.astype(BF16)

            @pl.when(jnp.logical_not(holds))
            def _():
                away = ring(x, 4 - y) - 1
                remote(
                    mids[t], narrows[t].at[away], bsend.at[t, 0], brecv.at[t, away], {"fsdp": y * 4 + z}
                ).start()

            return
        u, v, x_first = axes(t)
        for d in (1, 3, 2, 0):
            to = ring(u, d)
            total = grad[l, to, v].astype(F32) if x_first else grad[l, v, to].astype(F32)
            for k in range(3):
                total = total + wides[t][k, to].astype(F32)
            mids[t][to] = total.astype(BF16)
            if d:
                k = NEAR.index(d)
                remote(
                    mids[t].at[to], narrows[t].at[k], bsend.at[t, k], brecv.at[t, k],
                    {"fsdp": joined(to, v, x_first)},
                ).start()

    def narrow_end(t):
        if t == 4:

            @pl.when(holds)
            def _():
                total = mids[t][...].astype(F32)
                for k in range(3):
                    remote(narrows[t].at[k], narrows[t].at[k], bsend.at[t, 0], brecv.at[t, k], sibling).wait_recv()
                    total = total + narrows[t][k].astype(F32)
                out_d[...] = total.astype(BF16)
                for k, d in enumerate(NEAR):
                    remote(out_d, out_d, ysend.at[t, k], yrecv.at[t, 0], {"seq": ring(y, d)}).start()

            return
        u, v, x_first = axes(t)
        total = mids[t][u].astype(F32)
        for k in range(3):
            remote(narrows[t].at[k], narrows[t].at[k], bsend.at[t, k], brecv.at[t, k], sibling).wait_recv()
            total = total + narrows[t][k].astype(F32)
        outs[t][y] = total.astype(BF16)
        for k, d in enumerate(NEAR):
            remote(
                outs[t].at[y], outs[t].at[y], ysend.at[t, k], yrecv.at[t, k], {"seq": ring(y, d)}
            ).start()

    def hidden_back(l):
        out_grad = dyall[l]
        return (dot_nt(out_grad, ws[l]) * slopes[l]).astype(BF16)

    def hidden_weights(l, hidden_grad):
        out_grad = dyall[l]
        keep(2, l, dot_tn(acts[l], out_grad))
        keep(1, l, dot_tn(n2s[l], hidden_grad))
        keep(4, l, dot_tn(ctx[l], out_grad))

    def attention_back(l):
        ctx_grad = dot_nt(dyall[l], wd[l]).astype(BF16)
        parts = ([], [], [])
        for n in range(3):
            q = qkvs[l, :, n * HD : (n + 1) * HD]
            k = qkvs[l, :, GROUP + n * HD : GROUP + (n + 1) * HD]
            v = qkvs[l, :, 2 * GROUP + n * HD : 2 * GROUP + (n + 1) * HD]
            up = ctx_grad[:, n * HD : (n + 1) * HD]
            prob = probs[l, n]
            prob_grad = dot_nt(up, v)
            inner = jnp.sum(prob * prob_grad, axis=-1, keepdims=True)
            score_grad = (prob * (prob_grad - inner)).astype(BF16)
            parts[0].append(dot(score_grad, k) * HD**-0.5)
            parts[1].append(dot_tn(score_grad, q) * HD**-0.5)
            parts[2].append(dot_tn(prob.astype(BF16), up))
        turned_grad = jnp.concatenate(parts[0] + parts[1], axis=1).astype(BF16).astype(F32)
        return jnp.concatenate(
            [turn(turned_grad, turn_tables(tab_ref, odd, -1))] + parts[2], axis=1
        ).astype(BF16)

    def vector_grads(l, hidden_grad, joint_grad, n1_grad, n2_grad):
        normed = xhs[l]
        grows[...] = jnp.zeros_like(grows)
        grows[0:1, :] = jnp.sum(n1_grad * normed, axis=0, keepdims=True)
        grows[1:2, :] = jnp.sum(n1_grad, axis=0, keepdims=True)
        grows[2:3, :] = jnp.sum(n2_grad * normed, axis=0, keepdims=True)
        grows[3:4, :] = jnp.sum(n2_grad, axis=0, keepdims=True)
        grows[4:5, :] = jnp.sum(dyall[l, own, :].astype(F32), axis=0, keepdims=True)
        grows[6:7, :] = jnp.sum(hidden_grad.astype(F32), axis=0, keepdims=True)
        joint_bias = jnp.sum(joint_grad.astype(F32), axis=0, keepdims=True)
        spread = spread_matrix()
        first = jnp.where(piece_mask((LEN, WIDTH)), jnp.concatenate([grows[...]] * 16, axis=0), 0.0)
        second = jnp.where(
            joint_mask((LEN, 3 * GROUP), y), jnp.broadcast_to(joint_bias, (LEN, 3 * GROUP)), 0.0
        )
        keep(
            3,
            l,
            dot_nt(first.astype(BF16), spread) + dot_nt(second.astype(BF16), spread[:, : 3 * GROUP]),
        )

    def backward_end(l):
        total = reduce_end(1, l)
        values = xall[l, own, :].astype(F32)
        center = values - jnp.mean(values, axis=-1, keepdims=True)
        scale = lax.rsqrt(jnp.mean(center * center, axis=-1, keepdims=True) + 1e-5)
        near = center * scale
        pulled = scale * (
            total
            - jnp.mean(total, axis=-1, keepdims=True)
            - near * jnp.mean(total * near, axis=-1, keepdims=True)
        )
        return (dyall[l, own, :].astype(F32) + pulled).astype(BF16)

    forward(0)
    middle = forward_end(0)
    xall[1, own, :] = middle
    share(xall.at[1], asend.at[0, 1], arecv.at[0, 1])
    staged[0, 0] = middle
    forward(1)

    collect(dyall.at[1], asend.at[1, 1], arecv.at[1, 1])
    hidden_grad = hidden_back(1)
    n2_grad = dot_nt(hidden_grad, we[1])
    joint_grad = attention_back(1)
    n1_grad = dot_nt(joint_grad, wq[1])
    reduce_start(n1_grad * vrows[1, 0:1, :] + n2_grad * vrows[1, 2:3, :], 1, 1)
    hidden_weights(1, hidden_grad)
    keep(0, 1, dot_tn(n1s[1], joint_grad))
    vector_grads(1, hidden_grad, joint_grad, n1_grad, n2_grad)
    staged[0, 1] = forward_end(1)
    upper = backward_end(1)
    dyall[0, own, :] = upper
    share(dyall.at[0], asend.at[1, 0], arecv.at[1, 0])
    staged[1, 1] = upper
    remote(staged.at[0, 1 - micro], lo_out.at[micro], osend.at[0], orecv.at[0], sibling).start()

    @pl.when(micro == 1)
    def _():
        for t in BACK:
            fold(t, 1)

    collect(dyall.at[0], asend.at[1, 0], arecv.at[1, 0])
    hidden_grad = hidden_back(0)
    hidden_weights(0, hidden_grad)
    joint_grad = attention_back(0)
    keep(0, 0, dot_tn(n1s[0], joint_grad))
    n1_grad = dot_nt(joint_grad, wq[0])
    n2_grad = dot_nt(hidden_grad, we[0])
    reduce_start(n1_grad * vrows[0, 0:1, :] + n2_grad * vrows[0, 2:3, :], 1, 0)
    vector_grads(0, hidden_grad, joint_grad, n1_grad, n2_grad)

    @pl.when(micro == 0)
    def _():
        for t in BACK:
            fold(t, 0)

    @pl.when(micro == 1)
    def _():
        for t in BACK:
            wide_end(t, 1)

    staged[1, 0] = backward_end(0)
    remote(staged.at[1, 1 - micro], ig_out.at[micro], osend.at[1], orecv.at[1], sibling).start()
    lo_out[micro] = staged[0, micro]
    ig_out[micro] = staged[1, micro]

    @pl.when(micro == 0)
    def _():
        for t in BACK:
            wide_end(t, 0)

    for t in BACK:
        narrow_end(t)

    for t in range(4):
        for k, d in enumerate(NEAR):
            src = outs[t].at[ring(y, 4 - d)]
            remote(src, src, ysend.at[t, k], yrecv.at[t, k], sibling).wait_recv()
            remote(src, src, ysend.at[t, k], yrecv.at[t, k], sibling).wait_send()
            remote(narrows[t].at[k], narrows[t].at[k], bsend.at[t, k], brecv.at[t, k], sibling).wait_send()
        for k in range(15):
            remote(shards[t], shards[t], gsend.at[t, k], grecv.at[t, 0], sibling).wait_send()
    for t in range(5):
        for k in range(3):
            remote(wides[t].at[k], wides[t].at[k], wsend.at[t, k], wrecv.at[t, k], sibling).wait_send()
        remote(wholes[t].at[0], wholes[t].at[0], csend.at[t], crecv.at[t], sibling).wait_send()
        remote(helds[t], helds[t], hsend.at[t], hrecv.at[t], sibling).wait_send()

    @pl.when(holds)
    def _():
        for k in range(3):
            remote(out_d, out_d, ysend.at[4, k], yrecv.at[4, 0], sibling).wait_send()
            remote(dw.at[0], dw.at[0], dsend.at[k], drecv.at[0], sibling).wait_send()

    @pl.when(jnp.logical_not(holds))
    def _():
        remote(out_d, out_d, ysend.at[4, 0], yrecv.at[4, 0], sibling).wait_recv()
        remote(md, md, bsend.at[4, 0], brecv.at[4, 0], sibling).wait_send()

    for k in range(3):
        remote(band(0, 0), band(0, 0), dsend.at[3 + k], drecv.at[0], sibling).wait_send()
        remote(posall.at[own, :], posall.at[own, :], posend.at[k], porecv.at[k], sibling).wait_send()
        for l in range(2):
            for back in range(2):
                src = xall.at[0, own, :]
                remote(src, src, asend.at[back, l, k], arecv.at[back, l, k], sibling).wait_send()
                src = prec.at[back, l, k]
                remote(src, src, rsend.at[back, l, k], rrecv.at[back, l, k], sibling).wait_send()
    for i, ref in enumerate((lo_out, ig_out)):
        remote(ref.at[0], ref.at[0], osend.at[i], orecv.at[i], sibling).wait()


def run_program(tokens, cot, positions, tables, vectors, weights):
    vmem = pl.BlockSpec(memory_space=pltpu.VMEM)
    dma = pltpu.SemaphoreType.DMA
    sizes = [(rows, cols) for rows, cols, _ in KINDS]

    def stacks(lead, dense_lead):
        return [pltpu.VMEM((*lead, rows, cols), BF16) for rows, cols in sizes] + [
            pltpu.VMEM((*dense_lead, 48, WIDTH), BF16)
        ]

    return pl.pallas_call(
        program_kernel,
        out_shape=[jax.ShapeDtypeStruct((4, rows, cols), BF16) for rows, cols in sizes]
        + [jax.ShapeDtypeStruct((48, WIDTH), BF16)]
        + [jax.ShapeDtypeStruct((2, TOK, WIDTH), BF16)] * 2,
        in_specs=[vmem] * 16,
        out_specs=[vmem] * 7,
        scratch_shapes=[
            pltpu.VMEM((48, 3 * GROUP), BF16),
            pltpu.VMEM((48, WIDTH), BF16),
            pltpu.VMEM((16, 128), BF16),
            pltpu.VMEM((16, 128), F32),
        ]
        + [pltpu.VMEM((2, 16 * rows, cols), BF16) for rows, cols in sizes]
        + [pltpu.VMEM((2, GROUP, WIDTH), BF16)]
        + stacks((2, 4, 4), (2, 4))
        + stacks((4, 4), (4,))
        + stacks((3, 4), (3,))
        + stacks((4,), ())
        + stacks((3,), (3,))
        + [
            pltpu.VMEM((2, LEN, WIDTH), BF16),
            pltpu.VMEM((2, LEN, WIDTH), BF16),
            pltpu.VMEM((LEN, 128), F32),
            pltpu.VMEM((2, 2, LEN, WIDTH), F32),
            pltpu.VMEM((2, 2, LEN, WIDTH), BF16),
            pltpu.VMEM((2, 2, 3, TOK, WIDTH), BF16),
            pltpu.VMEM((2, LEN, 3 * GROUP), BF16),
            pltpu.VMEM((2, 3, LEN, LEN), F32),
            pltpu.VMEM((2, LEN, GROUP), BF16),
            pltpu.VMEM((2, LEN, WIDTH), BF16),
            pltpu.VMEM((2, LEN, WIDTH), F32),
            pltpu.VMEM((2, LEN, WIDTH), BF16),
            pltpu.VMEM((2, LEN, WIDTH), BF16),
            pltpu.VMEM((2, LEN, WIDTH), F32),
            pltpu.VMEM((2, 16, WIDTH), F32),
            pltpu.VMEM((2, 8, 3 * GROUP), F32),
            pltpu.VMEM((16, WIDTH), F32),
            pltpu.VMEM((2, 2, TOK, WIDTH), BF16),
            dma((4, 15)),
            dma((4, 16)),
            dma((6,)),
            dma((4,)),
            dma((5,)),
            dma((5,)),
            dma((2, 2, 3)),
            dma((2, 2, 3)),
            dma((2, 2, 3)),
            dma((2, 2, 3)),
            dma((3,)),
            dma((3,)),
            dma((5,)),
            dma((5,)),
            dma((5, 3)),
            dma((5, 3)),
            dma((5, 3)),
            dma((5, 3)),
            dma((5, 3)),
            dma((5, 3)),
            dma((2,)),
            dma((2,)),
        ],
        compiler_params=pltpu.CompilerParams(
            collective_id=1, has_side_effects=True, vmem_limit_bytes=58 * MIB
        ),
        name="layers",
    )(tokens, cot, positions, tables, *vectors, *weights)


def lay_out_kernel(
    q, e, s, v, d, lo, ig,
    lo_out, ig_out, o0, o1, o2, o3, q_out, qb_out, d_out, db_out, e_out, eb_out, s_out, sb_out,
):
    lo_out[...] = lo[...]
    ig_out[...] = ig[...]
    for t in range(3):
        for h in range(4):
            at = WIDTH * t + GROUP * h
            q_out[0, :, at : at + GROUP] = q[h, :, GROUP * t : GROUP * (t + 1)].astype(F32)
    for f in range(0, 16, 2):
        e_out[0, :, GROUP * f : GROUP * (f + 2)] = jnp.concatenate(
            [e[h, :, 48 * i : 48 * i + 48].astype(F32) for i in (f, f + 1) for h in range(4)], axis=1
        )
    for h in range(4):
        s_out[0, 48 * h : 48 * h + 48, :] = s[h].astype(F32)
    d_out[0] = d[...].astype(F32)
    total = v[0].astype(F32) + v[1].astype(F32) + v[2].astype(F32) + v[3].astype(F32)
    for i, ref in enumerate((o0, o1, o2, o3, db_out)):
        ref[...] = total[i : i + 1, 0:48]
    sb_out[...] = total[4:5, 0:48]
    qb_out[...] = jnp.concatenate([total[7 + k : 8 + k, 0:48] for k in range(3)], axis=1)
    eb_out[...] = jnp.concatenate([v[h].astype(F32)[6:7, 0:48] for h in range(4)], axis=1)


def lay_out(parts):
    vmem = pl.BlockSpec(memory_space=pltpu.VMEM)
    flat = jax.ShapeDtypeStruct((1, 48), F32)
    rows = jax.ShapeDtypeStruct((2, TOK, WIDTH), BF16)

    def wide(height, width):
        return jax.ShapeDtypeStruct((1, height, width), F32)

    shapes = [
        rows, rows, flat, flat, flat, flat, wide(48, 3 * WIDTH), jax.ShapeDtypeStruct((1, 144), F32),
        wide(48, WIDTH), flat, wide(48, 4 * WIDTH), jax.ShapeDtypeStruct((1, GROUP), F32),
        wide(GROUP, WIDTH), flat,
    ]
    return pl.pallas_call(
        lay_out_kernel,
        out_shape=shapes,
        in_specs=[vmem] * 7,
        out_specs=[vmem] * 14,
        compiler_params=pltpu.CompilerParams(vmem_limit_bytes=32 * MIB),
        name="lay_out",
    )(*parts)


def angle_tables():
    lane = np.arange(128) % HD
    frequency = np.exp(-math.log(10000.0) * (2.0 / ROT) * np.arange(ROT // 2)).astype(np.float32)
    tables = []
    for offset in (0, 1):
        spots = (2 * np.arange(LEN) + offset).astype(np.float32)
        angle = (spots[:, None] * frequency[None, :])[:, lane % 8].astype(np.float64)
        cosine = np.where(lane < ROT, np.cos(angle), 1.0)
        low_sine = np.where(lane < 8, -np.sin(angle), 0.0)
        high_sine = np.where((lane >= 8) & (lane < ROT), np.sin(angle), 0.0)
        tables += [cosine, low_sine, high_sine]
    return np.stack(tables).astype(np.float32)


def on_device(
    tokens_in, cotangent, positions, first_gain, first_bias, second_gain, second_bias,
    qkv_weight, qkv_bias, dense_weight, dense_bias, expand_weight, expand_bias,
    shrink_weight, shrink_bias,
):
    parts = run_program(
        tokens_in,
        cotangent,
        positions,
        jnp.asarray(angle_tables()),
        (first_gain, first_bias, second_gain, second_bias, dense_bias, shrink_bias, qkv_bias, expand_bias),
        (qkv_weight, expand_weight, shrink_weight, dense_weight),
    )
    layer_out, input_grad, *rest = lay_out(parts)
    shape = (1, 2, 1, TOK, WIDTH)
    return (layer_out.reshape(shape), input_grad.reshape(shape), *rest)


def solution(mesh):
    tokens = P(None, "fsdp", "seq", None)
    flat = P("section", "fsdp")
    wide = P("section", "fsdp", None)
    out = P("section", None, "fsdp", "seq", None)
    return jax.shard_map(
        on_device,
        mesh=mesh,
        in_specs=(
            tokens, tokens, P(None, "fsdp", "seq"), flat, flat, flat, flat,
            wide, flat, wide, flat, wide, flat, wide, flat,
        ),
        out_specs=(
            out, out, flat, flat, flat, flat, wide, flat, wide, flat, wide, flat, wide, flat,
        ),
        check_vma=False,
    )
```

```python
import math

import jax
import jax.numpy as jnp
import numpy as np
from jax import lax
from jax.experimental import pallas as pl
from jax.experimental.pallas import tpu as pltpu
from jax.sharding import PartitionSpec as P

MESH = pl.DeviceIdType.MESH
F32 = jnp.float32
BF16 = jnp.bfloat16
HD = 64
ROT = 16
WIDTH = 768
TOK = 64
HALF = 32
SPLIT = 128
LEN = 256
GROUP = 192
NEAR = (1, 3, 2)
PARTS = (0, 1)
MIB = 1024 * 1024

KINDS = ((48, 576, False), (48, 768, True), (48, 768, False), (16, 128, True))


def ring(value, by):
    return lax.rem(value + by, 4)


def places():
    owner = lax.axis_index("fsdp")
    return owner, lax.div(owner, 4), lax.rem(owner, 4)


def joined(u, v, x_first):
    return u * 4 + v if x_first else v * 4 + u


def remote(src, dst, send, recv, target):
    return pltpu.make_async_remote_copy(
        src_ref=src, dst_ref=dst, send_sem=send, recv_sem=recv, device_id=target, device_id_type=MESH
    )


def greet(targets):
    barrier = pltpu.get_barrier_semaphore()
    for target in targets:
        pl.semaphore_signal(barrier, inc=1, device_id=target, device_id_type=MESH)
    pl.semaphore_wait(barrier, len(targets))


def sheet_peers(x, z):
    return [{"fsdp": ring(x, d) * 4 + z} for d in (1, 2, 3)] + [
        {"fsdp": x * 4 + ring(z, d)} for d in (1, 2, 3)
    ]


def seq_peers(y):
    return [{"seq": ring(y, d)} for d in (1, 2, 3)]


def dot(a, b):
    return jnp.dot(a, b, preferred_element_type=F32)


def dot_nt(a, b):
    return lax.dot_general(a, b, (((1,), (1,)), ((), ())), preferred_element_type=F32)


def dot_tn(a, b):
    return lax.dot_general(a, b, (((0,), (0,)), ((), ())), preferred_element_type=F32)


def turn_tables(tab_ref, odd, sign):
    tables = []
    for i in range(3):
        table = jnp.where(odd, tab_ref[3 + i], tab_ref[i])
        if i and sign < 0:
            table = -table
        tables.append(jnp.concatenate([table] * 3, axis=1))
    return tables


def turn(values, tables):
    cosine, low_sine, high_sine = tables
    span = values.shape[1]
    return (
        values * cosine
        + pltpu.roll(values, span - 8, 1) * low_sine
        + pltpu.roll(values, 8, 1) * high_sine
    )


def pieces_of(h):
    chunks = [16 * t + 4 * h + i for t in range(3) for i in range(4)]
    return [(chunk // 3, chunk % 3) for chunk in chunks]


ORDER = (0, 3, 1, 2)
BACK = (2, 1, 4, 0, 3)


def program_kernel(*refs):
    (
        x_ref, cot_ref, pos_ref, tab_hbm, fg, fb, sg, sb, db, hb, qb, eb, q_hbm, e_hbm, s_hbm, d_hbm,
        out_q, out_e, out_s, out_v, out_d, lo_out, ig_out,
        tab_ref, qw, ew, qs, es, vs, vecf, wq, we, ws, wv, wd,
        dq, de, ds, dv, dd, hq, he, hs, hv, hd, aq, ae, as_, av, ad,
        fq, fe, fs, pq, pe, ps, mq, me, ms, mv, md, nq, ne, ns, nv, nd,
        xall, dyall, posall, part, psend, prec, qkvs, probs, ctx, acts, slopes,
        n1s, n2s, xhs, vrows, bqs, grows, staged, end_e, lsem,
        gsend, grecv, dsend, drecv, csend, crecv,
        asend, arecv, rsend, rrecv, posend, porecv,
        hsend, hrecv, wsend, wrecv, bsend, brecv, ysend, yrecv, osend, orecv,
    ) = refs
    micro = lax.axis_index("section")
    y = lax.axis_index("seq")
    owner, x, z = places()
    sibling = {"section": 1 - micro}
    holds = x == y

    def piece(i, a):
        return pl.ds(pl.multiple_of(a * SPLIT + i * HALF, HALF), HALF)

    peers = sheet_peers(x, z) + seq_peers(y) + [sibling]
    peers += [{"seq": ring(y, d), "section": 1 - micro} for d in (1, 2, 3)]
    barrier = pltpu.get_barrier_semaphore()
    for target in peers:
        pl.semaphore_signal(barrier, inc=1, device_id=target, device_id_type=MESH)

    def mine(rows):
        return pl.ds(pl.multiple_of(owner * rows, 16), rows)

    def band(l, i):
        return wd.at[l, pl.ds(pl.multiple_of(i * 48, 16), 48), :]

    shrink_rows = s_hbm.at[0, pl.ds(pl.multiple_of(48 * y, 16), 48), :]
    loads = [
        pltpu.make_async_copy(src, dst, lsem.at[i])
        for i, (src, dst) in enumerate(
            [(q_hbm.at[0], qw), (e_hbm.at[0], ew), (shrink_rows, ws.at[micro, mine(48), :])]
            + [(x_ref.at[micro, 0, HALF * a : HALF * (a + 1), :], xall.at[0, piece(y, a), :]) for a in PARTS]
            + [(cot_ref.at[micro, 0, HALF * a : HALF * (a + 1), :], dyall.at[1, piece(y, a), :]) for a in PARTS]
            + [(tab_hbm, tab_ref), (d_hbm.at[0], band(micro, z))]
        )
    ]
    for load in loads[:-1]:
        load.start()

    @pl.when(holds)
    def _():
        loads[-1].start()

    vecf[...] = jnp.zeros_like(vecf)
    for i, ref in enumerate((fg, fb, sg, sb, db, hb)):
        vecf[i : i + 1, 0:48] = ref[...].astype(F32)
    for k in range(3):
        vecf[7 + k : 8 + k, 0:48] = qb[:, 48 * k : 48 * k + 48].astype(F32)
    loads[0].wait()
    loads[1].wait()
    for h in range(4):

        @pl.when(y == h)
        def _():
            qs[...] = jnp.concatenate(
                [qw[:, WIDTH * t + GROUP * h : WIDTH * t + GROUP * (h + 1)] for t in range(3)], axis=1
            )
            es[...] = jnp.concatenate(
                [ew[:, GROUP * f + 48 * h : GROUP * f + 48 * h + 48] for f in range(16)], axis=1
            )
            vecf[6:7, 0:48] = eb[:, 48 * h : 48 * h + 48].astype(F32)

    vs[...] = vecf[...].astype(BF16)
    wholes = (wq, we, ws, wv, wd)

    def slot(t, l, s):
        rows = KINDS[t][0]
        return wholes[t].at[l, pl.ds(pl.multiple_of(s * rows, 16), rows), :]

    wq[micro, mine(48), :] = qs[...]
    we[micro, mine(48), :] = es[...]
    wv[micro, mine(16), :] = vs[...]
    shape = (TOK, TOK)
    level = lax.broadcasted_iota(jnp.int32, shape, 0) == lax.broadcasted_iota(jnp.int32, shape, 1)
    spots = jnp.where(level, jnp.broadcast_to(pos_ref[micro].astype(F32), shape), 0.0)
    spots = jnp.broadcast_to(jnp.sum(spots, axis=1, keepdims=True), (TOK, 128))
    for a in PARTS:
        posall[piece(y, a), :] = spots[HALF * a : HALF * (a + 1)]
    for load in loads[2:-1]:
        load.wait()

    @pl.when(holds)
    def _():
        loads[-1].wait()

    pl.semaphore_wait(barrier, len(peers))

    def axes(t, l):
        x_first = KINDS[t][2] ^ (l == 1)
        return (x, z, x_first) if x_first else (z, x, x_first)

    def gather_start(l):
        for t in ORDER:
            u, v, x_first = axes(t, l)
            for k, d in enumerate(NEAR):
                remote(
                    slot(t, l, owner), slot(t, l, owner), gsend.at[t, k], grecv.at[t, owner],
                    {"fsdp": joined(ring(u, d), v, x_first)},
                ).start()

        @pl.when(holds)
        def _():
            for k, d in enumerate(NEAR):
                remote(
                    band(l, z), band(l, z), dsend.at[k], drecv.at[z], {"fsdp": ring(x, d) * 4 + z}
                ).start()

    def gather_forward(l):
        for t, d in [(t, d) for d in (0, 1, 3, 2) for t in (0, 1)] + [(t, d) for t in (3, 2) for d in (0, 1, 3, 2)]:
            u, v, x_first = axes(t, l)
            s = joined(ring(u, 4 - d), v, x_first)
            if d:
                remote(slot(t, l, s), slot(t, l, s), gsend.at[t, 0], grecv.at[t, s], sibling).wait_recv()
            for k, e in enumerate(NEAR if t == 3 else (1, 3)):
                remote(
                    slot(t, l, s), slot(t, l, s), gsend.at[t, (3 + 3 * d if t == 3 else 3 + 2 * d) + k],
                    grecv.at[t, s], {"fsdp": joined(u, ring(v, e), x_first)},
                ).start()

        @pl.when(jnp.logical_not(holds))
        def _():
            remote(band(l, z), band(l, z), dsend.at[0], drecv.at[z], sibling).wait_recv()

        for k, e in enumerate(NEAR):
            remote(
                band(l, z), band(l, z), dsend.at[3 + k], drecv.at[z], {"fsdp": x * 4 + ring(z, e)}
            ).start()

    def gather_relay(l):
        for t in (0, 1, 2):
            u, v, x_first = axes(t, l)
            for w in (0, 2, 1, 3):
                back, ahead = (3, 1) if w < 2 else (1, 3)
                s = joined(w, ring(v, back), x_first)
                remote(slot(t, l, s), slot(t, l, s), gsend.at[t, 0], grecv.at[t, s], sibling).wait_recv()
                remote(
                    slot(t, l, s), slot(t, l, s), gsend.at[t, 11 + w], grecv.at[t, s],
                    {"fsdp": joined(u, ring(v, ahead), x_first)},
                ).start()

    def need(t, l):
        @pl.when(micro == l)
        def _():
            if t < 4:
                u, v, x_first = axes(t, l)
                for e, w in [(e, w) for e in NEAR for w in range(4)]:
                    if t == 3 or e == 2 or (w < 2) == (e == 3):
                        s = joined(w, ring(v, 4 - e), x_first)
                        remote(slot(t, l, s), slot(t, l, s), gsend.at[t, 0], grecv.at[t, s], sibling).wait_recv()
            else:
                for e in NEAR:
                    i = ring(z, 4 - e)
                    remote(band(l, i), band(l, i), dsend.at[0], drecv.at[i], sibling).wait_recv()
            remote(wholes[t].at[l], wholes[t].at[l], csend.at[t], crecv.at[t], sibling).start()

        @pl.when(micro != l)
        def _():
            remote(wholes[t].at[l], wholes[t].at[l], csend.at[t], crecv.at[t], sibling).wait_recv()

    def share(ref, a, sends, recvs):
        src = ref.at[piece(y, a), :]
        for k, d in enumerate(NEAR):
            remote(src, src, sends.at[a, k], recvs.at[a, k], {"seq": ring(y, d)}).start()

    def collect(ref, a, sends, recvs):
        for k, d in enumerate(NEAR):
            src = ref.at[piece(ring(y, 4 - d), a), :]
            remote(src, src, sends.at[a, k], recvs.at[a, k], sibling).wait_recv()

    def reduce_start(value, a, back, l):
        rows = slice(a * SPLIT, (a + 1) * SPLIT)
        part[back, l, rows] = value
        psend[back, l, rows] = value.astype(BF16)
        for k, d in enumerate(NEAR):
            to = ring(y, d)
            remote(
                psend.at[back, l, piece(to, a), :], prec.at[back, l, a, k],
                rsend.at[back, l, a, k], rrecv.at[back, l, a, k], {"seq": to},
            ).start()

    def reduce_end(a, back, l):
        total = part[back, l, piece(y, a), :]
        for k in range(3):
            remote(
                prec.at[back, l, a, k], prec.at[back, l, a, k],
                rsend.at[back, l, a, k], rrecv.at[back, l, a, k], sibling,
            ).wait_recv()
            total = total + prec[back, l, a, k].astype(F32)
        return total

    for a in PARTS:
        share(xall.at[0], a, asend.at[0, 0], arecv.at[0, 0])
        share(posall, a, posend, porecv)

    @pl.when(micro == 0)
    def _():
        gather_start(0)

    for a in PARTS:
        share(dyall.at[1], a, asend.at[1, 1], arecv.at[1, 1])

    @pl.when(micro == 0)
    def _():
        gather_forward(0)
        gather_relay(0)

    for a in PARTS:
        collect(posall, a, posend, porecv)

    def token_of(row):
        return (
            (lax.shift_right_logical(row, 5) & 3) * TOK + lax.shift_right_logical(row, 7) * HALF + (row & 31)
        )

    token = token_of(lax.broadcasted_iota(jnp.int32, (LEN, 128), 0))
    odd = posall[...] > (2 * token).astype(F32) + 0.5

    def forward(l):
        need(3, l)
        vrows[l] = jnp.concatenate(
            [wv[l, 16 * f : 16 * f + 16, 0:48].astype(F32) for f in range(16)], axis=1
        )
        for h in range(4):

            @pl.when(y == h)
            def _():
                bqs[l, 0:1, :] = jnp.concatenate(
                    [vrows[l, 7 + k : 8 + k, 48 * f : 48 * f + 48] for f, k in pieces_of(h)], axis=1
                )

        tables = turn_tables(tab_ref, odd, 1)
        for a in PARTS:
            rows = slice(a * SPLIT, (a + 1) * SPLIT)
            collect(xall.at[l], a, asend.at[0, l], arecv.at[0, l])
            values = xall[l, rows].astype(F32)
            center = values - jnp.mean(values, axis=-1, keepdims=True)
            scale = lax.rsqrt(jnp.mean(center * center, axis=-1, keepdims=True) + 1e-5)
            normed = center * scale
            xhs[l, rows] = normed
            n1 = (normed * vrows[l, 0:1, :] + vrows[l, 1:2, :]).astype(BF16)
            n1s[l, rows] = n1
            n2s[l, rows] = (normed * vrows[l, 2:3, :] + vrows[l, 3:4, :]).astype(BF16)
            if a == 0:
                need(0, l)
                if l == 0:

                    @pl.when(micro == 1)
                    def _():
                        gather_start(1)

            joint = dot(n1, wq[l]) + bqs[l, 0:1, :]
            turned = turn(joint[:, : 2 * GROUP], [table[rows] for table in tables])
            qkvs[l, rows, : 2 * GROUP] = turned.astype(BF16)
            qkvs[l, rows, 2 * GROUP :] = joint[:, 2 * GROUP :].astype(BF16)
        row = token_of(lax.broadcasted_iota(jnp.int32, (LEN, LEN), 0))
        allowed = row >= token_of(lax.broadcasted_iota(jnp.int32, (LEN, LEN), 1))
        for n in range(3):
            q = qkvs[l, :, n * HD : (n + 1) * HD]
            k = qkvs[l, :, GROUP + n * HD : GROUP + (n + 1) * HD]
            v = qkvs[l, :, 2 * GROUP + n * HD : 2 * GROUP + (n + 1) * HD]
            scores = jnp.where(allowed, dot_nt(q, k) * HD**-0.5, -1e30)
            powers = jnp.exp(scores - jnp.max(scores, axis=-1, keepdims=True))
            prob = powers / jnp.sum(powers, axis=-1, keepdims=True)
            probs[l, n] = prob
            ctx[l, :, n * HD : (n + 1) * HD] = dot(prob.astype(BF16), v).astype(BF16)
        if l == 0:

            @pl.when(micro == 1)
            def _():
                gather_forward(1)

        need(1, l)
        hidden = dot(n2s[l], we[l]) + vrows[l, 6:7, :]
        phi = 0.5 + 0.5 * lax.erf(hidden * math.sqrt(0.5))
        acts[l] = (hidden * phi).astype(BF16)
        need(4, l)
        need(2, l)
        for a in PARTS:
            rows = slice(a * SPLIT, (a + 1) * SPLIT)
            reduce_start(dot(ctx[l, rows], wd[l]) + dot(acts[l, rows], ws[l]), a, 0, l)
        density = jnp.exp(-0.5 * hidden * hidden) * (1.0 / math.sqrt(2.0 * math.pi))
        slopes[l] = phi + hidden * density

    def forward_end(a, l):
        total = reduce_end(a, 0, l)
        result = xall[l, piece(y, a), :].astype(F32) + total + vrows[l, 4:5, :] + vrows[l, 5:6, :]
        return result.astype(BF16)

    grads = (dq, de, ds, dv, dd)
    helds = (hq, he, hs, hv, hd)
    wides = (aq, ae, as_, av, ad)
    fars, passed = (fq, fe, fs), (pq, pe, ps)
    mids = (mq, me, ms, mv, md)
    narrows = (nq, ne, ns, nv, nd)
    outs = (out_q, out_e, out_s, out_v, out_d)

    def core_of(t, l):
        return 1 - l if t == 1 else l

    def on_core(todo, t, l):
        @pl.when(micro == core_of(t, l))
        def _():
            todo(t, l)

    def keep(t, l, value):
        rows = KINDS[t][0] if t < 4 else 48
        value = value.astype(BF16)
        for b in range(value.shape[0] // rows):
            piece = value[b * rows : (b + 1) * rows]
            if t < 4:
                grads[t][l, b // 4, b % 4] = piece
            else:
                grads[t][l, b] = piece

        @pl.when(micro != core_of(t, l))
        def _():
            remote(grads[t].at[l], helds[t], hsend.at[t], hrecv.at[t], sibling).start()

    def fold(t, l):
        remote(helds[t], helds[t], hsend.at[t], hrecv.at[t], sibling).wait_recv()
        grad, held = grads[t], helds[t]
        if t == 4:
            for i in range(4):
                grad[l, i] = (grad[l, i].astype(F32) + held[i].astype(F32)).astype(BF16)
            for k, e in enumerate(NEAR):
                to = ring(z, e)
                remote(
                    grad.at[l, to], wides[t].at[k], wsend.at[t, k], wrecv.at[t, k], {"fsdp": x * 4 + to}
                ).start()
            return

        def add(i, carry):
            a, b = lax.div(i, 4), lax.rem(i, 4)
            grad[l, a, b] = (grad[l, a, b].astype(F32) + held[a, b].astype(F32)).astype(BF16)
            return carry

        lax.fori_loop(0, 16, add, 0)
        u, v, x_first = axes(t, l)
        if t == 3:
            for k, e in enumerate(NEAR):
                to = ring(v, e)
                remote(
                    grad.at[l, :, to] if x_first else grad.at[l, to],
                    wides[t].at[k], wsend.at[t, k], wrecv.at[t, k], {"fsdp": joined(u, to, x_first)},
                ).start()
            return
        low, high = pl.ds(0, 2), pl.ds(2, 2)
        ahead, behind, across = ring(v, 1), ring(v, 3), ring(v, 2)
        for k, (half, to, dst, via) in enumerate(
            [
                (low, across, fars[t].at[0], ahead),
                (high, across, fars[t].at[1], behind),
                (high, ahead, wides[t].at[0, high], ahead),
                (low, behind, wides[t].at[1, low], behind),
            ]
        ):
            remote(
                grad.at[l, half, to] if x_first else grad.at[l, to, half],
                dst, wsend.at[t, k], wrecv.at[t, k], {"fsdp": joined(u, via, x_first)},
            ).start()

    def relay(t, l):
        grad = grads[t]
        u, v, x_first = axes(t, l)
        for i, to in enumerate((ring(v, 1), ring(v, 3))):
            remote(fars[t].at[i], fars[t].at[i], wsend.at[t, i], wrecv.at[t, i], sibling).wait_recv()
            for b in range(2):
                w = 2 * i + b
                near = grad[l, w, to] if x_first else grad[l, to, w]
                passed[t][i, b] = (near.astype(F32) + fars[t][i, b].astype(F32)).astype(BF16)
            remote(
                passed[t].at[i], wides[t].at[i, pl.ds(2 * i, 2)], wsend.at[t, 4 + i], wrecv.at[t, 4 + i],
                {"fsdp": joined(u, to, x_first)},
            ).start()

    def wide_end(t, l):
        grad = grads[t]
        terms = 3 if t > 2 else 2
        if t > 2:
            for k in range(3):
                remote(wides[t].at[k], wides[t].at[k], wsend.at[t, k], wrecv.at[t, k], sibling).wait_recv()
        else:
            for k, i in ((2, 0), (3, 1), (4, 0), (5, 1)):
                half = wides[t].at[i, pl.ds(0, 2)]
                remote(half, half, wsend.at[t, k], wrecv.at[t, k], sibling).wait_recv()
        if t == 4:
            total = grad[l, z].astype(F32)
            for k in range(3):
                total = total + wides[t][k].astype(F32)
            mids[t][...] = total.astype(BF16)

            @pl.when(jnp.logical_not(holds))
            def _():
                away = ring(x, 4 - y) - 1
                remote(
                    mids[t], narrows[t].at[away], bsend.at[t, 0], brecv.at[t, away], {"fsdp": y * 4 + z}
                ).start()

            return
        u, v, x_first = axes(t, l)
        for d in (1, 3, 2, 0):
            to = ring(u, d)
            total = grad[l, to, v].astype(F32) if x_first else grad[l, v, to].astype(F32)
            for k in range(terms):
                total = total + wides[t][k, to].astype(F32)
            mids[t][to] = total.astype(BF16)
            if d:
                k = NEAR.index(d)
                remote(
                    mids[t].at[to], narrows[t].at[k], bsend.at[t, k], brecv.at[t, k],
                    {"fsdp": joined(to, v, x_first)},
                ).start()

    def narrow_end(t, l):
        if t == 4:

            @pl.when(holds)
            def _():
                total = mids[t][...].astype(F32)
                for k in range(3):
                    remote(narrows[t].at[k], narrows[t].at[k], bsend.at[t, 0], brecv.at[t, k], sibling).wait_recv()
                    total = total + narrows[t][k].astype(F32)
                out_d[...] = total.astype(BF16)
                for k, d in enumerate(NEAR):
                    remote(out_d, out_d, ysend.at[t, k], yrecv.at[t, 0], {"seq": ring(y, d)}).start()

            return
        u, v, x_first = axes(t, l)
        total = mids[t][u].astype(F32)
        for k in range(3):
            remote(narrows[t].at[k], narrows[t].at[k], bsend.at[t, k], brecv.at[t, k], sibling).wait_recv()
            total = total + narrows[t][k].astype(F32)
        if t == 1:
            end_e[...] = total.astype(BF16)
            for k, d in enumerate(NEAR + (0,)):
                remote(
                    end_e, out_e.at[y], ysend.at[t, k], yrecv.at[t, k],
                    {"seq": ring(y, d), "section": 1 - micro},
                ).start()
            return
        outs[t][y] = total.astype(BF16)
        for k, d in enumerate(NEAR):
            remote(
                outs[t].at[y], outs[t].at[y], ysend.at[t, k], yrecv.at[t, k], {"seq": ring(y, d)}
            ).start()

    def arrive_back(l):
        pieces = []
        for a in PARTS:
            rows = slice(a * SPLIT, (a + 1) * SPLIT)
            collect(dyall.at[l], a, asend.at[1, l], arecv.at[1, l])
            out_grad = dyall[l, rows]
            pieces.append((dot_nt(out_grad, ws[l]) * slopes[l, rows]).astype(BF16))
        return jnp.concatenate(pieces, axis=0)

    def hidden_weights(l, hidden_grad):
        out_grad = dyall[l]
        keep(2, l, dot_tn(acts[l], out_grad))
        keep(1, l, dot_tn(n2s[l], hidden_grad))
        keep(4, l, dot_tn(ctx[l], out_grad))

    def attention_back(l):
        ctx_grad = dot_nt(dyall[l], wd[l]).astype(BF16)
        parts = ([], [], [])
        for n in range(3):
            q = qkvs[l, :, n * HD : (n + 1) * HD]
            k = qkvs[l, :, GROUP + n * HD : GROUP + (n + 1) * HD]
            v = qkvs[l, :, 2 * GROUP + n * HD : 2 * GROUP + (n + 1) * HD]
            up = ctx_grad[:, n * HD : (n + 1) * HD]
            prob = probs[l, n]
            prob_grad = dot_nt(up, v)
            inner = jnp.sum(prob * prob_grad, axis=-1, keepdims=True)
            score_grad = (prob * (prob_grad - inner)).astype(BF16)
            parts[0].append(dot(score_grad, k) * HD**-0.5)
            parts[1].append(dot_tn(score_grad, q) * HD**-0.5)
            parts[2].append(dot_tn(prob.astype(BF16), up))
        turned_grad = jnp.concatenate(parts[0] + parts[1], axis=1).astype(BF16).astype(F32)
        return jnp.concatenate(
            [turn(turned_grad, turn_tables(tab_ref, odd, -1))] + parts[2], axis=1
        ).astype(BF16)

    def vector_grads(l, hidden_grad, joint_grad, n1_grad, n2_grad):
        normed = xhs[l]
        grows[...] = jnp.zeros_like(grows)
        grows[0:1, :WIDTH] = jnp.sum(n1_grad * normed, axis=0, keepdims=True)
        grows[1:2, :WIDTH] = jnp.sum(n1_grad, axis=0, keepdims=True)
        grows[2:3, :WIDTH] = jnp.sum(n2_grad * normed, axis=0, keepdims=True)
        grows[3:4, :WIDTH] = jnp.sum(n2_grad, axis=0, keepdims=True)
        grows[4:5, :WIDTH] = sum(
            jnp.sum(dyall[l, piece(y, a), :].astype(F32), axis=0, keepdims=True) for a in PARTS
        )
        grows[6:7, :WIDTH] = jnp.sum(hidden_grad.astype(F32), axis=0, keepdims=True)
        joint_bias = jnp.sum(joint_grad.astype(F32), axis=0, keepdims=True)
        for h in range(4):

            @pl.when(y == h)
            def _():
                for i, (f, k) in enumerate(pieces_of(h)):
                    grows[7 + k : 8 + k, 48 * f : 48 * f + 48] = joint_bias[:, 48 * i : 48 * i + 48]

        keep(3, l, jnp.concatenate([grows[:, 48 * f : 48 * f + 128] for f in range(16)], axis=0))

    def backward_end(a, l):
        total = reduce_end(a, 1, l)
        values = xall[l, piece(y, a), :].astype(F32)
        center = values - jnp.mean(values, axis=-1, keepdims=True)
        scale = lax.rsqrt(jnp.mean(center * center, axis=-1, keepdims=True) + 1e-5)
        near = center * scale
        pulled = scale * (
            total
            - jnp.mean(total, axis=-1, keepdims=True)
            - near * jnp.mean(total * near, axis=-1, keepdims=True)
        )
        return (dyall[l, piece(y, a), :].astype(F32) + pulled).astype(BF16)

    def norm_back(l, hidden_grad, joint_grad):
        n1_grads, n2_grads = [], []
        for a in PARTS:
            rows = slice(a * SPLIT, (a + 1) * SPLIT)
            n1_grads.append(dot_nt(joint_grad[rows], wq[l]))
            n2_grads.append(dot_nt(hidden_grad[rows], we[l]))
            reduce_start(n1_grads[a] * vrows[l, 0:1, :] + n2_grads[a] * vrows[l, 2:3, :], a, 1, l)
        return jnp.concatenate(n1_grads, axis=0), jnp.concatenate(n2_grads, axis=0)

    forward(0)

    @pl.when(micro == 1)
    def _():
        gather_relay(1)

    for a in PARTS:
        middle = forward_end(a, 0)
        xall[1, piece(y, a), :] = middle
        share(xall.at[1], a, asend.at[0, 1], arecv.at[0, 1])
        staged[0, 0, HALF * a : HALF * (a + 1), :] = middle
    forward(1)

    hidden_grad = arrive_back(1)
    hidden_weights(1, hidden_grad)
    joint_grad = attention_back(1)
    n1_grad, n2_grad = norm_back(1, hidden_grad, joint_grad)
    keep(0, 1, dot_tn(n1s[1], joint_grad))
    for t in (2, 1, 4, 0):
        on_core(fold, t, 1)
    for a in PARTS:
        upper = backward_end(a, 1)
        dyall[0, piece(y, a), :] = upper
        share(dyall.at[0], a, asend.at[1, 0], arecv.at[1, 0])
        staged[1, 1, HALF * a : HALF * (a + 1), :] = upper
    vector_grads(1, hidden_grad, joint_grad, n1_grad, n2_grad)
    on_core(fold, 3, 1)
    for t in (2, 1, 0):
        on_core(relay, t, 1)
    for a in PARTS:
        staged[0, 1, HALF * a : HALF * (a + 1), :] = forward_end(a, 1)
    remote(staged.at[0, 1 - micro], lo_out.at[micro], osend.at[0], orecv.at[0], sibling).start()

    hidden_grad = arrive_back(0)
    hidden_weights(0, hidden_grad)
    joint_grad = attention_back(0)
    keep(0, 0, dot_tn(n1s[0], joint_grad))
    for t in (2, 1, 4):
        on_core(fold, t, 0)
    for t in BACK:
        on_core(wide_end, t, 1)
    n1_grad, n2_grad = norm_back(0, hidden_grad, joint_grad)
    on_core(fold, 0, 0)
    vector_grads(0, hidden_grad, joint_grad, n1_grad, n2_grad)
    on_core(fold, 3, 0)
    for t in BACK:
        on_core(narrow_end, t, 1)
    for t in (2, 1):
        on_core(relay, t, 0)
    for a in PARTS:
        staged[1, 0, HALF * a : HALF * (a + 1), :] = backward_end(a, 0)
    remote(staged.at[1, 1 - micro], ig_out.at[micro], osend.at[1], orecv.at[1], sibling).start()
    lo_out[micro] = staged[0, micro]
    ig_out[micro] = staged[1, micro]
    on_core(relay, 0, 0)
    for t in (4, 2, 1, 3, 0):
        on_core(wide_end, t, 0)
    for t in (4, 2, 1, 3, 0):
        on_core(narrow_end, t, 0)

    remote(end_e, out_e.at[y], ysend.at[1, 3], yrecv.at[1, 3], sibling).wait()
    for t in range(4):
        for k, d in enumerate(NEAR):
            src = outs[t].at[ring(y, 4 - d)]
            remote(src, src, ysend.at[t, k], yrecv.at[t, k], sibling).wait_recv()
            remote(src, src, ysend.at[t, k], yrecv.at[t, k], sibling).wait_send()
            remote(narrows[t].at[k], narrows[t].at[k], bsend.at[t, k], brecv.at[t, k], sibling).wait_send()
        for k in range(15):
            remote(slot(t, 0, 0), slot(t, 0, 0), gsend.at[t, k], grecv.at[t, 0], sibling).wait_send()
    for t in range(5):
        for k in range(6 if t < 3 else 3):
            src = wides[t].at[0, pl.ds(0, 2)] if t < 3 else wides[t].at[0]
            remote(src, src, wsend.at[t, k], wrecv.at[t, k], sibling).wait_send()
        remote(wholes[t].at[0], wholes[t].at[0], csend.at[t], crecv.at[t], sibling).wait_send()
        remote(helds[t], helds[t], hsend.at[t], hrecv.at[t], sibling).wait_send()

    @pl.when(holds)
    def _():
        for k in range(3):
            remote(out_d, out_d, ysend.at[4, k], yrecv.at[4, 0], sibling).wait_send()
            remote(band(0, 0), band(0, 0), dsend.at[k], drecv.at[0], sibling).wait_send()

    @pl.when(jnp.logical_not(holds))
    def _():
        remote(out_d, out_d, ysend.at[4, 0], yrecv.at[4, 0], sibling).wait_recv()
        remote(md, md, bsend.at[4, 0], brecv.at[4, 0], sibling).wait_send()

    for k in range(3):
        remote(band(0, 0), band(0, 0), dsend.at[3 + k], drecv.at[0], sibling).wait_send()
        for a in PARTS:
            src = posall.at[piece(y, a), :]
            remote(src, src, posend.at[a, k], porecv.at[a, k], sibling).wait_send()
            for l in range(2):
                for back in range(2):
                    src = xall.at[0, piece(y, a), :]
                    remote(src, src, asend.at[back, l, a, k], arecv.at[back, l, a, k], sibling).wait_send()
                    src = prec.at[back, l, a, k]
                    remote(src, src, rsend.at[back, l, a, k], rrecv.at[back, l, a, k], sibling).wait_send()
    for i, ref in enumerate((lo_out, ig_out)):
        remote(ref.at[0], ref.at[0], osend.at[i], orecv.at[i], sibling).wait()


def run_program(tokens, cot, positions, tables, vectors, weights):
    vmem = pl.BlockSpec(memory_space=pltpu.VMEM)
    hbm = pl.BlockSpec(memory_space=pl.ANY)
    dma = pltpu.SemaphoreType.DMA
    sizes = [(rows, cols) for rows, cols, _ in KINDS]

    def stacks(lead, dense_lead):
        return [pltpu.VMEM((*lead, rows, cols), BF16) for rows, cols in sizes] + [
            pltpu.VMEM((*dense_lead, 48, WIDTH), BF16)
        ]

    return pl.pallas_call(
        program_kernel,
        out_shape=[jax.ShapeDtypeStruct((4, rows, cols), BF16) for rows, cols in sizes]
        + [jax.ShapeDtypeStruct((48, WIDTH), BF16)]
        + [jax.ShapeDtypeStruct((2, TOK, WIDTH), BF16)] * 2,
        in_specs=[hbm, hbm, vmem, hbm] + [vmem] * 8 + [hbm] * 4,
        out_specs=[vmem] * 7,
        scratch_shapes=[
            pltpu.VMEM((6, LEN, 128), F32),
            pltpu.VMEM((48, 3 * WIDTH), BF16),
            pltpu.VMEM((48, 4 * WIDTH), BF16),
            pltpu.VMEM((48, 3 * GROUP), BF16),
            pltpu.VMEM((48, WIDTH), BF16),
            pltpu.VMEM((16, 128), BF16),
            pltpu.VMEM((16, 128), F32),
        ]
        + [pltpu.VMEM((2, 16 * rows, cols), BF16) for rows, cols in sizes]
        + [pltpu.VMEM((2, GROUP, WIDTH), BF16)]
        + stacks((2, 4, 4), (2, 4))
        + stacks((4, 4), (4,))
        + [pltpu.VMEM((2 if rows == 48 else 3, 4, rows, cols), BF16) for rows, cols in sizes]
        + [pltpu.VMEM((3, 48, WIDTH), BF16)]
        + [pltpu.VMEM((2, 2, rows, cols), BF16) for rows, cols in sizes[:3]] * 2
        + stacks((4,), ())
        + stacks((3,), (3,))
        + [
            pltpu.VMEM((2, LEN, WIDTH), BF16),
            pltpu.VMEM((2, LEN, WIDTH), BF16),
            pltpu.VMEM((LEN, 128), F32),
            pltpu.VMEM((2, 2, LEN, WIDTH), F32),
            pltpu.VMEM((2, 2, LEN, WIDTH), BF16),
            pltpu.VMEM((2, 2, 2, 3, HALF, WIDTH), BF16),
            pltpu.VMEM((2, LEN, 3 * GROUP), BF16),
            pltpu.VMEM((2, 3, LEN, LEN), F32),
            pltpu.VMEM((2, LEN, GROUP), BF16),
            pltpu.VMEM((2, LEN, WIDTH), BF16),
            pltpu.VMEM((2, LEN, WIDTH), F32),
            pltpu.VMEM((2, LEN, WIDTH), BF16),
            pltpu.VMEM((2, LEN, WIDTH), BF16),
            pltpu.VMEM((2, LEN, WIDTH), F32),
            pltpu.VMEM((2, 16, WIDTH), F32),
            pltpu.VMEM((2, 8, 3 * GROUP), F32),
            pltpu.VMEM((16, WIDTH + 128), F32),
            pltpu.VMEM((2, 2, TOK, WIDTH), BF16),
            pltpu.VMEM((48, WIDTH), BF16),
            dma((9,)),
            dma((4, 15)),
            dma((4, 16)),
            dma((6,)),
            dma((4,)),
            dma((5,)),
            dma((5,)),
            dma((2, 2, 2, 3)),
            dma((2, 2, 2, 3)),
            dma((2, 2, 2, 3)),
            dma((2, 2, 2, 3)),
            dma((2, 3)),
            dma((2, 3)),
            dma((5,)),
            dma((5,)),
            dma((5, 6)),
            dma((5, 6)),
            dma((5, 3)),
            dma((5, 3)),
            dma((5, 4)),
            dma((5, 4)),
            dma((2,)),
            dma((2,)),
        ],
        compiler_params=pltpu.CompilerParams(
            collective_id=1, has_side_effects=True, vmem_limit_bytes=58 * MIB
        ),
        name="layers",
    )(tokens, cot, positions, tables, *vectors, *weights)


def lay_out_kernel(
    q, e, s, v, d, lo, ig,
    lo_out, ig_out, o0, o1, o2, o3, q_out, qb_out, d_out, db_out, e_out, eb_out, s_out, sb_out,
):
    lo_out[...] = lo[...]
    ig_out[...] = ig[...]
    for t in range(3):
        for h in range(4):
            at = WIDTH * t + GROUP * h
            q_out[0, :, at : at + GROUP] = q[h, :, GROUP * t : GROUP * (t + 1)].astype(F32)
    for f in range(0, 16, 2):
        e_out[0, :, GROUP * f : GROUP * (f + 2)] = jnp.concatenate(
            [e[h, :, 48 * i : 48 * i + 48].astype(F32) for i in (f, f + 1) for h in range(4)], axis=1
        )
    for h in range(4):
        s_out[0, 48 * h : 48 * h + 48, :] = s[h].astype(F32)
    d_out[0] = d[...].astype(F32)
    total = v[0].astype(F32) + v[1].astype(F32) + v[2].astype(F32) + v[3].astype(F32)
    for i, ref in enumerate((o0, o1, o2, o3, db_out)):
        ref[...] = total[i : i + 1, 0:48]
    sb_out[...] = total[4:5, 0:48]
    qb_out[...] = jnp.concatenate([total[7 + k : 8 + k, 0:48] for k in range(3)], axis=1)
    eb_out[...] = jnp.concatenate([v[h].astype(F32)[6:7, 0:48] for h in range(4)], axis=1)


def lay_out(parts):
    vmem = pl.BlockSpec(memory_space=pltpu.VMEM)
    flat = jax.ShapeDtypeStruct((1, 48), F32)
    rows = jax.ShapeDtypeStruct((2, TOK, WIDTH), BF16)

    def wide(height, width):
        return jax.ShapeDtypeStruct((1, height, width), F32)

    shapes = [
        rows, rows, flat, flat, flat, flat, wide(48, 3 * WIDTH), jax.ShapeDtypeStruct((1, 144), F32),
        wide(48, WIDTH), flat, wide(48, 4 * WIDTH), jax.ShapeDtypeStruct((1, GROUP), F32),
        wide(GROUP, WIDTH), flat,
    ]
    return pl.pallas_call(
        lay_out_kernel,
        out_shape=shapes,
        in_specs=[vmem] * 7,
        out_specs=[vmem] * 14,
        compiler_params=pltpu.CompilerParams(vmem_limit_bytes=62 * MIB),
        name="lay_out",
    )(*parts)


def angle_tables():
    lane = np.arange(128) % HD
    frequency = np.exp(-math.log(10000.0) * (2.0 / ROT) * np.arange(ROT // 2)).astype(np.float32)
    tables = []
    for offset in (0, 1):
        row = np.arange(LEN)
        token = (row // HALF % 4) * TOK + row // SPLIT * HALF + row % HALF
        spots = (2 * token + offset).astype(np.float32)
        angle = (spots[:, None] * frequency[None, :])[:, lane % 8].astype(np.float64)
        cosine = np.where(lane < ROT, np.cos(angle), 1.0)
        low_sine = np.where(lane < 8, -np.sin(angle), 0.0)
        high_sine = np.where((lane >= 8) & (lane < ROT), np.sin(angle), 0.0)
        tables += [cosine, low_sine, high_sine]
    return np.stack(tables).astype(np.float32)


def on_device(
    tokens_in, cotangent, positions, first_gain, first_bias, second_gain, second_bias,
    qkv_weight, qkv_bias, dense_weight, dense_bias, expand_weight, expand_bias,
    shrink_weight, shrink_bias,
):
    parts = run_program(
        tokens_in,
        cotangent,
        positions,
        jnp.asarray(angle_tables()),
        (first_gain, first_bias, second_gain, second_bias, dense_bias, shrink_bias, qkv_bias, expand_bias),
        (qkv_weight, expand_weight, shrink_weight, dense_weight),
    )
    layer_out, input_grad, *rest = lay_out(parts)
    shape = (1, 2, 1, TOK, WIDTH)
    return (layer_out.reshape(shape), input_grad.reshape(shape), *rest)


def solution(mesh):
    tokens = P(None, "fsdp", "seq", None)
    flat = P("section", "fsdp")
    wide = P("section", "fsdp", None)
    out = P("section", None, "fsdp", "seq", None)
    return jax.shard_map(
        on_device,
        mesh=mesh,
        in_specs=(
            tokens, tokens, P(None, "fsdp", "seq"), flat, flat, flat, flat,
            wide, flat, wide, flat, wide, flat, wide, flat,
        ),
        out_specs=(
            out, out, flat, flat, flat, flat, wide, flat, wide, flat, wide, flat, wide, flat,
        ),
        check_vma=False,
    )
```

```python
import math

import jax
import jax.numpy as jnp
import numpy as np
from jax import lax
from jax.experimental import pallas as pl
from jax.experimental.pallas import tpu as pltpu
from jax.sharding import PartitionSpec as P

MESH = pl.DeviceIdType.MESH
F32 = jnp.float32
BF16 = jnp.bfloat16
HD = 64
ROT = 16
WIDTH = 768
TOK = 64
HALF = 32
SPLIT = 128
LEN = 256
GROUP = 192
NEAR = (1, 3, 2)
PARTS = (0, 1)
MIB = 1024 * 1024

KINDS = ((48, 576, False), (48, 768, True), (48, 768, False), (16, 128, True))


def ring(value, by):
    return lax.rem(value + by, 4)


def places():
    owner = lax.axis_index("fsdp")
    return owner, lax.div(owner, 4), lax.rem(owner, 4)


def joined(u, v, x_first):
    return u * 4 + v if x_first else v * 4 + u


def remote(src, dst, send, recv, target):
    return pltpu.make_async_remote_copy(
        src_ref=src, dst_ref=dst, send_sem=send, recv_sem=recv, device_id=target, device_id_type=MESH
    )


def greet(targets):
    barrier = pltpu.get_barrier_semaphore()
    for target in targets:
        pl.semaphore_signal(barrier, inc=1, device_id=target, device_id_type=MESH)
    pl.semaphore_wait(barrier, len(targets))


def sheet_peers(x, z):
    return [{"fsdp": ring(x, d) * 4 + z} for d in (1, 2, 3)] + [
        {"fsdp": x * 4 + ring(z, d)} for d in (1, 2, 3)
    ]


def seq_peers(y):
    return [{"seq": ring(y, d)} for d in (1, 2, 3)]


def dot(a, b):
    return jnp.dot(a, b, preferred_element_type=F32)


def dot_nt(a, b):
    return lax.dot_general(a, b, (((1,), (1,)), ((), ())), preferred_element_type=F32)


def dot_tn(a, b):
    return lax.dot_general(a, b, (((0,), (0,)), ((), ())), preferred_element_type=F32)


def turn_tables(tab_ref, odd, sign):
    tables = []
    for i in range(3):
        table = jnp.where(odd, tab_ref[3 + i], tab_ref[i])
        if i and sign < 0:
            table = -table
        tables.append(jnp.concatenate([table] * 3, axis=1))
    return tables


def turn(values, tables):
    cosine, low_sine, high_sine = tables
    span = values.shape[1]
    return (
        values * cosine
        + pltpu.roll(values, span - 8, 1) * low_sine
        + pltpu.roll(values, 8, 1) * high_sine
    )


def pieces_of(h):
    chunks = [16 * t + 4 * h + i for t in range(3) for i in range(4)]
    return [(chunk // 3, chunk % 3) for chunk in chunks]


ORDER = (0, 3, 1, 2)
BACK = (2, 1, 4, 0, 3)


def program_kernel(*refs):
    (
        x_ref, cot_ref, pos_ref, tab_hbm, fg, fb, sg, sb, db, hb, qb, eb, q_hbm, e_hbm, s_hbm, d_hbm,
        out_q, out_e, out_s, out_v, out_d, lo_out, ig_out,
        tab_ref, qw, ew, qs, es, vs, vecf, wq, we, ws, wv, wd,
        dq, de, ds, dv, dd, hq, he, hs, hv, hd, aq, ae, as_, av, ad,
        fq, fe, fs, pq, pe, ps, mq, me, ms, mv, md, nq, ne, ns, nv, nd,
        xall, dyall, posall, part, psend, prec, qkvs, probs, ctx, acts, slopes,
        n1s, n2s, xhs, vrows, bqs, grows, staged, end_e, lsem,
        gsend, grecv, dsend, drecv, csend, crecv,
        asend, arecv, rsend, rrecv, posend, porecv,
        hsend, hrecv, wsend, wrecv, bsend, brecv, ysend, yrecv, osend, orecv,
    ) = refs
    micro = lax.axis_index("section")
    y = lax.axis_index("seq")
    owner, x, z = places()
    sibling = {"section": 1 - micro}
    holds = x == y

    def piece(i, a):
        return pl.ds(pl.multiple_of(a * SPLIT + i * HALF, HALF), HALF)

    peers = sheet_peers(x, z) + seq_peers(y) + [sibling]
    peers += [{"seq": ring(y, d), "section": 1 - micro} for d in (1, 2, 3)]
    barrier = pltpu.get_barrier_semaphore()
    for target in peers:
        pl.semaphore_signal(barrier, inc=1, device_id=target, device_id_type=MESH)

    def mine(rows):
        return pl.ds(pl.multiple_of(owner * rows, 16), rows)

    def band(l, i):
        return wd.at[l, pl.ds(pl.multiple_of(i * 48, 16), 48), :]

    shrink_rows = s_hbm.at[0, pl.ds(pl.multiple_of(48 * y, 16), 48), :]
    loads = [
        pltpu.make_async_copy(src, dst, lsem.at[i])
        for i, (src, dst) in enumerate(
            [(q_hbm.at[0], qw), (e_hbm.at[0], ew), (shrink_rows, ws.at[micro, mine(48), :])]
            + [(x_ref.at[micro, 0, HALF * a : HALF * (a + 1), :], xall.at[0, piece(y, a), :]) for a in PARTS]
            + [(cot_ref.at[micro, 0, HALF * a : HALF * (a + 1), :], dyall.at[1, piece(y, a), :]) for a in PARTS]
            + [(tab_hbm, tab_ref), (d_hbm.at[0], band(micro, z))]
        )
    ]
    for load in loads[:-1]:
        load.start()

    @pl.when(holds)
    def _():
        loads[-1].start()

    vecf[...] = jnp.zeros_like(vecf)
    for i, ref in enumerate((fg, fb, sg, sb, db, hb)):
        vecf[i : i + 1, 0:48] = ref[...].astype(F32)
    for k in range(3):
        vecf[7 + k : 8 + k, 0:48] = qb[:, 48 * k : 48 * k + 48].astype(F32)
    loads[0].wait()
    loads[1].wait()
    for h in range(4):

        @pl.when(y == h)
        def _():
            qs[...] = jnp.concatenate(
                [qw[:, WIDTH * t + GROUP * h : WIDTH * t + GROUP * (h + 1)] for t in range(3)], axis=1
            )
            es[...] = jnp.concatenate(
                [ew[:, GROUP * f + 48 * h : GROUP * f + 48 * h + 48] for f in range(16)], axis=1
            )
            vecf[6:7, 0:48] = eb[:, 48 * h : 48 * h + 48].astype(F32)

    vs[...] = vecf[...].astype(BF16)
    wholes = (wq, we, ws, wv, wd)

    def slot(t, l, s):
        rows = KINDS[t][0]
        return wholes[t].at[l, pl.ds(pl.multiple_of(s * rows, 16), rows), :]

    wq[micro, mine(48), :] = qs[...]
    we[micro, mine(48), :] = es[...]
    wv[micro, mine(16), :] = vs[...]
    shape = (TOK, TOK)
    level = lax.broadcasted_iota(jnp.int32, shape, 0) == lax.broadcasted_iota(jnp.int32, shape, 1)
    spots = jnp.where(level, jnp.broadcast_to(pos_ref[micro].astype(F32), shape), 0.0)
    spots = jnp.broadcast_to(jnp.sum(spots, axis=1, keepdims=True), (TOK, 128))
    for a in PARTS:
        posall[piece(y, a), :] = spots[HALF * a : HALF * (a + 1)]
    for load in loads[2:-1]:
        load.wait()

    @pl.when(holds)
    def _():
        loads[-1].wait()

    pl.semaphore_wait(barrier, len(peers))

    def axes(t, l):
        x_first = KINDS[t][2] ^ (l == 1)
        return (x, z, x_first) if x_first else (z, x, x_first)

    def gather_start(l):
        for t in ORDER:
            u, v, x_first = axes(t, l)
            for k, d in enumerate(NEAR):
                remote(
                    slot(t, l, owner), slot(t, l, owner), gsend.at[t, k], grecv.at[t, owner],
                    {"fsdp": joined(ring(u, d), v, x_first)},
                ).start()

        @pl.when(holds)
        def _():
            for k, d in enumerate(NEAR):
                remote(
                    band(l, z), band(l, z), dsend.at[k], drecv.at[z], {"fsdp": ring(x, d) * 4 + z}
                ).start()

    def gather_forward(l):
        for t, d in [(t, d) for d in (0, 1, 3, 2) for t in (0, 1)] + [(t, d) for t in (3, 2) for d in (0, 1, 3, 2)]:
            u, v, x_first = axes(t, l)
            s = joined(ring(u, 4 - d), v, x_first)
            if d:
                remote(slot(t, l, s), slot(t, l, s), gsend.at[t, 0], grecv.at[t, s], sibling).wait_recv()
            for k, e in enumerate(NEAR if t == 3 else (1, 3)):
                remote(
                    slot(t, l, s), slot(t, l, s), gsend.at[t, (3 + 3 * d if t == 3 else 3 + 2 * d) + k],
                    grecv.at[t, s], {"fsdp": joined(u, ring(v, e), x_first)},
                ).start()

        @pl.when(jnp.logical_not(holds))
        def _():
            remote(band(l, z), band(l, z), dsend.at[0], drecv.at[z], sibling).wait_recv()

        for k, e in enumerate(NEAR):
            remote(
                band(l, z), band(l, z), dsend.at[3 + k], drecv.at[z], {"fsdp": x * 4 + ring(z, e)}
            ).start()

    def gather_relay(l):
        for t in (0, 1, 2):
            u, v, x_first = axes(t, l)
            for w in (0, 2, 1, 3):
                back, ahead = (3, 1) if w < 2 else (1, 3)
                s = joined(w, ring(v, back), x_first)
                remote(slot(t, l, s), slot(t, l, s), gsend.at[t, 0], grecv.at[t, s], sibling).wait_recv()
                remote(
                    slot(t, l, s), slot(t, l, s), gsend.at[t, 11 + w], grecv.at[t, s],
                    {"fsdp": joined(u, ring(v, ahead), x_first)},
                ).start()

    def need(t, l):
        @pl.when(micro == l)
        def _():
            if t < 4:
                u, v, x_first = axes(t, l)
                for e, w in [(e, w) for e in NEAR for w in range(4)]:
                    if t == 3 or e == 2 or (w < 2) == (e == 3):
                        s = joined(w, ring(v, 4 - e), x_first)
                        remote(slot(t, l, s), slot(t, l, s), gsend.at[t, 0], grecv.at[t, s], sibling).wait_recv()
            else:
                for e in NEAR:
                    i = ring(z, 4 - e)
                    remote(band(l, i), band(l, i), dsend.at[0], drecv.at[i], sibling).wait_recv()
            remote(wholes[t].at[l], wholes[t].at[l], csend.at[t], crecv.at[t], sibling).start()

        @pl.when(micro != l)
        def _():
            remote(wholes[t].at[l], wholes[t].at[l], csend.at[t], crecv.at[t], sibling).wait_recv()

    def share(ref, a, sends, recvs):
        src = ref.at[piece(y, a), :]
        for k, d in enumerate(NEAR):
            remote(src, src, sends.at[a, k], recvs.at[a, k], {"seq": ring(y, d)}).start()

    def collect(ref, a, sends, recvs):
        for k, d in enumerate(NEAR):
            src = ref.at[piece(ring(y, 4 - d), a), :]
            remote(src, src, sends.at[a, k], recvs.at[a, k], sibling).wait_recv()

    def reduce_start(value, a, back, l):
        rows = slice(a * SPLIT, (a + 1) * SPLIT)
        part[back, l, rows] = value
        psend[back, l, rows] = value.astype(BF16)
        for k, d in enumerate(NEAR):
            to = ring(y, d)
            remote(
                psend.at[back, l, piece(to, a), :], prec.at[back, l, a, k],
                rsend.at[back, l, a, k], rrecv.at[back, l, a, k], {"seq": to},
            ).start()

    def reduce_end(a, back, l):
        total = part[back, l, piece(y, a), :]
        for k in range(3):
            remote(
                prec.at[back, l, a, k], prec.at[back, l, a, k],
                rsend.at[back, l, a, k], rrecv.at[back, l, a, k], sibling,
            ).wait_recv()
            total = total + prec[back, l, a, k].astype(F32)
        return total

    @pl.when(micro == 0)
    def _():
        gather_start(0)

    for a in PARTS:
        share(xall.at[0], a, asend.at[0, 0], arecv.at[0, 0])
        share(posall, a, posend, porecv)

    @pl.when(micro == 0)
    def _():
        gather_forward(0)
        gather_relay(0)

    for a in PARTS:
        share(dyall.at[1], a, asend.at[1, 1], arecv.at[1, 1])
    for a in PARTS:
        collect(posall, a, posend, porecv)

    def token_of(row):
        return (
            (lax.shift_right_logical(row, 5) & 3) * TOK + lax.shift_right_logical(row, 7) * HALF + (row & 31)
        )

    token = token_of(lax.broadcasted_iota(jnp.int32, (LEN, 128), 0))
    odd = posall[...] > (2 * token).astype(F32) + 0.5

    def forward(l):
        need(3, l)
        vrows[l] = jnp.concatenate(
            [wv[l, 16 * f : 16 * f + 16, 0:48].astype(F32) for f in range(16)], axis=1
        )
        for h in range(4):

            @pl.when(y == h)
            def _():
                bqs[l, 0:1, :] = jnp.concatenate(
                    [vrows[l, 7 + k : 8 + k, 48 * f : 48 * f + 48] for f, k in pieces_of(h)], axis=1
                )

        tables = turn_tables(tab_ref, odd, 1)
        for a in PARTS:
            rows = slice(a * SPLIT, (a + 1) * SPLIT)
            collect(xall.at[l], a, asend.at[0, l], arecv.at[0, l])
            values = xall[l, rows].astype(F32)
            center = values - jnp.mean(values, axis=-1, keepdims=True)
            scale = lax.rsqrt(jnp.mean(center * center, axis=-1, keepdims=True) + 1e-5)
            normed = center * scale
            xhs[l, rows] = normed
            n1 = (normed * vrows[l, 0:1, :] + vrows[l, 1:2, :]).astype(BF16)
            n1s[l, rows] = n1
            n2s[l, rows] = (normed * vrows[l, 2:3, :] + vrows[l, 3:4, :]).astype(BF16)
            if a == 0:
                need(0, l)
                if l == 0:

                    @pl.when(micro == 1)
                    def _():
                        gather_start(1)

            joint = dot(n1, wq[l]) + bqs[l, 0:1, :]
            turned = turn(joint[:, : 2 * GROUP], [table[rows] for table in tables])
            qkvs[l, rows, : 2 * GROUP] = turned.astype(BF16)
            qkvs[l, rows, 2 * GROUP :] = joint[:, 2 * GROUP :].astype(BF16)
        row = token_of(lax.broadcasted_iota(jnp.int32, (LEN, LEN), 0))
        allowed = row >= token_of(lax.broadcasted_iota(jnp.int32, (LEN, LEN), 1))
        for n in range(3):
            q = qkvs[l, :, n * HD : (n + 1) * HD]
            k = qkvs[l, :, GROUP + n * HD : GROUP + (n + 1) * HD]
            v = qkvs[l, :, 2 * GROUP + n * HD : 2 * GROUP + (n + 1) * HD]
            scores = jnp.where(allowed, dot_nt(q, k) * HD**-0.5, -1e30)
            powers = jnp.exp(scores - jnp.max(scores, axis=-1, keepdims=True))
            prob = powers / jnp.sum(powers, axis=-1, keepdims=True)
            probs[l, n] = prob
            ctx[l, :, n * HD : (n + 1) * HD] = dot(prob.astype(BF16), v).astype(BF16)
        if l == 0:

            @pl.when(micro == 1)
            def _():
                gather_forward(1)

        need(1, l)
        hidden = dot(n2s[l], we[l]) + vrows[l, 6:7, :]
        phi = 0.5 + 0.5 * lax.erf(hidden * math.sqrt(0.5))
        acts[l] = (hidden * phi).astype(BF16)
        need(4, l)
        need(2, l)
        for a in PARTS:
            rows = slice(a * SPLIT, (a + 1) * SPLIT)
            reduce_start(dot(ctx[l, rows], wd[l]) + dot(acts[l, rows], ws[l]), a, 0, l)
        density = jnp.exp(-0.5 * hidden * hidden) * (1.0 / math.sqrt(2.0 * math.pi))
        slopes[l] = phi + hidden * density

    def forward_end(a, l):
        total = reduce_end(a, 0, l)
        result = xall[l, piece(y, a), :].astype(F32) + total + vrows[l, 4:5, :] + vrows[l, 5:6, :]
        return result.astype(BF16)

    grads = (dq, de, ds, dv, dd)
    helds = (hq, he, hs, hv, hd)
    wides = (aq, ae, as_, av, ad)
    fars, passed = (fq, fe, fs), (pq, pe, ps)
    mids = (mq, me, ms, mv, md)
    narrows = (nq, ne, ns, nv, nd)
    outs = (out_q, out_e, out_s, out_v, out_d)

    def core_of(t, l):
        return 1 - l if t == 1 else l

    def on_core(todo, t, l):
        @pl.when(micro == core_of(t, l))
        def _():
            todo(t, l)

    def keep(t, l, value):
        rows = KINDS[t][0] if t < 4 else 48
        value = value.astype(BF16)
        for b in range(value.shape[0] // rows):
            piece = value[b * rows : (b + 1) * rows]
            if t < 4:
                grads[t][l, b // 4, b % 4] = piece
            else:
                grads[t][l, b] = piece

        @pl.when(micro != core_of(t, l))
        def _():
            remote(grads[t].at[l], helds[t], hsend.at[t], hrecv.at[t], sibling).start()

    def fold(t, l):
        remote(helds[t], helds[t], hsend.at[t], hrecv.at[t], sibling).wait_recv()
        grad, held = grads[t], helds[t]
        if t == 4:
            for i in range(4):
                grad[l, i] = (grad[l, i].astype(F32) + held[i].astype(F32)).astype(BF16)
            for k, e in enumerate(NEAR):
                to = ring(z, e)
                remote(
                    grad.at[l, to], wides[t].at[k], wsend.at[t, k], wrecv.at[t, k], {"fsdp": x * 4 + to}
                ).start()
            return

        def add(i, carry):
            a, b = lax.div(i, 4), lax.rem(i, 4)
            grad[l, a, b] = (grad[l, a, b].astype(F32) + held[a, b].astype(F32)).astype(BF16)
            return carry

        lax.fori_loop(0, 16, add, 0)
        u, v, x_first = axes(t, l)
        if t == 3:
            for k, e in enumerate(NEAR):
                to = ring(v, e)
                remote(
                    grad.at[l, :, to] if x_first else grad.at[l, to],
                    wides[t].at[k], wsend.at[t, k], wrecv.at[t, k], {"fsdp": joined(u, to, x_first)},
                ).start()
            return
        low, high = pl.ds(0, 2), pl.ds(2, 2)
        ahead, behind, across = ring(v, 1), ring(v, 3), ring(v, 2)
        for k, (half, to, dst, via) in enumerate(
            [
                (low, across, fars[t].at[0], ahead),
                (high, across, fars[t].at[1], behind),
                (high, ahead, wides[t].at[0, high], ahead),
                (low, behind, wides[t].at[1, low], behind),
            ]
        ):
            remote(
                grad.at[l, half, to] if x_first else grad.at[l, to, half],
                dst, wsend.at[t, k], wrecv.at[t, k], {"fsdp": joined(u, via, x_first)},
            ).start()

    def relay(t, l):
        grad = grads[t]
        u, v, x_first = axes(t, l)
        for i, to in enumerate((ring(v, 1), ring(v, 3))):
            remote(fars[t].at[i], fars[t].at[i], wsend.at[t, i], wrecv.at[t, i], sibling).wait_recv()
            for b in range(2):
                w = 2 * i + b
                near = grad[l, w, to] if x_first else grad[l, to, w]
                passed[t][i, b] = (near.astype(F32) + fars[t][i, b].astype(F32)).astype(BF16)
            remote(
                passed[t].at[i], wides[t].at[i, pl.ds(2 * i, 2)], wsend.at[t, 4 + i], wrecv.at[t, 4 + i],
                {"fsdp": joined(u, to, x_first)},
            ).start()

    def wide_end(t, l):
        grad = grads[t]
        terms = 3 if t > 2 else 2
        if t > 2:
            for k in range(3):
                remote(wides[t].at[k], wides[t].at[k], wsend.at[t, k], wrecv.at[t, k], sibling).wait_recv()
        else:
            for k, i in ((2, 0), (3, 1), (4, 0), (5, 1)):
                half = wides[t].at[i, pl.ds(0, 2)]
                remote(half, half, wsend.at[t, k], wrecv.at[t, k], sibling).wait_recv()
        if t == 4:
            total = grad[l, z].astype(F32)
            for k in range(3):
                total = total + wides[t][k].astype(F32)
            mids[t][...] = total.astype(BF16)

            @pl.when(jnp.logical_not(holds))
            def _():
                away = ring(x, 4 - y) - 1
                remote(
                    mids[t], narrows[t].at[away], bsend.at[t, 0], brecv.at[t, away], {"fsdp": y * 4 + z}
                ).start()

            return
        u, v, x_first = axes(t, l)
        for d in (1, 3, 2, 0):
            to = ring(u, d)
            total = grad[l, to, v].astype(F32) if x_first else grad[l, v, to].astype(F32)
            for k in range(terms):
                total = total + wides[t][k, to].astype(F32)
            mids[t][to] = total.astype(BF16)
            if d:
                k = NEAR.index(d)
                remote(
                    mids[t].at[to], narrows[t].at[k], bsend.at[t, k], brecv.at[t, k],
                    {"fsdp": joined(to, v, x_first)},
                ).start()

    def narrow_end(t, l):
        if t == 4:

            @pl.when(holds)
            def _():
                total = mids[t][...].astype(F32)
                for k in range(3):
                    remote(narrows[t].at[k], narrows[t].at[k], bsend.at[t, 0], brecv.at[t, k], sibling).wait_recv()
                    total = total + narrows[t][k].astype(F32)
                out_d[...] = total.astype(BF16)
                for k, d in enumerate(NEAR):
                    remote(out_d, out_d, ysend.at[t, k], yrecv.at[t, 0], {"seq": ring(y, d)}).start()

            return
        u, v, x_first = axes(t, l)
        total = mids[t][u].astype(F32)
        for k in range(3):
            remote(narrows[t].at[k], narrows[t].at[k], bsend.at[t, k], brecv.at[t, k], sibling).wait_recv()
            total = total + narrows[t][k].astype(F32)
        if t == 1:
            end_e[...] = total.astype(BF16)
            for k, d in enumerate(NEAR + (0,)):
                remote(
                    end_e, out_e.at[y], ysend.at[t, k], yrecv.at[t, k],
                    {"seq": ring(y, d), "section": 1 - micro},
                ).start()
            return
        outs[t][y] = total.astype(BF16)
        for k, d in enumerate(NEAR):
            remote(
                outs[t].at[y], outs[t].at[y], ysend.at[t, k], yrecv.at[t, k], {"seq": ring(y, d)}
            ).start()

    def arrive_back(l):
        pieces = []
        for a in PARTS:
            rows = slice(a * SPLIT, (a + 1) * SPLIT)
            collect(dyall.at[l], a, asend.at[1, l], arecv.at[1, l])
            out_grad = dyall[l, rows]
            pieces.append((dot_nt(out_grad, ws[l]) * slopes[l, rows]).astype(BF16))
        return jnp.concatenate(pieces, axis=0)

    def hidden_weights(l, hidden_grad):
        out_grad = dyall[l]
        keep(2, l, dot_tn(acts[l], out_grad))
        keep(1, l, dot_tn(n2s[l], hidden_grad))
        keep(4, l, dot_tn(ctx[l], out_grad))

    def attention_back(l):
        ctx_grad = dot_nt(dyall[l], wd[l]).astype(BF16)
        parts = ([], [], [])
        for n in range(3):
            q = qkvs[l, :, n * HD : (n + 1) * HD]
            k = qkvs[l, :, GROUP + n * HD : GROUP + (n + 1) * HD]
            v = qkvs[l, :, 2 * GROUP + n * HD : 2 * GROUP + (n + 1) * HD]
            up = ctx_grad[:, n * HD : (n + 1) * HD]
            prob = probs[l, n]
            prob_grad = dot_nt(up, v)
            inner = jnp.sum(prob * prob_grad, axis=-1, keepdims=True)
            score_grad = (prob * (prob_grad - inner)).astype(BF16)
            parts[0].append(dot(score_grad, k) * HD**-0.5)
            parts[1].append(dot_tn(score_grad, q) * HD**-0.5)
            parts[2].append(dot_tn(prob.astype(BF16), up))
        turned_grad = jnp.concatenate(parts[0] + parts[1], axis=1).astype(BF16).astype(F32)
        return jnp.concatenate(
            [turn(turned_grad, turn_tables(tab_ref, odd, -1))] + parts[2], axis=1
        ).astype(BF16)

    def vector_grads(l, hidden_grad, joint_grad, n1_grad, n2_grad):
        normed = xhs[l]
        grows[...] = jnp.zeros_like(grows)
        grows[0:1, :WIDTH] = jnp.sum(n1_grad * normed, axis=0, keepdims=True)
        grows[1:2, :WIDTH] = jnp.sum(n1_grad, axis=0, keepdims=True)
        grows[2:3, :WIDTH] = jnp.sum(n2_grad * normed, axis=0, keepdims=True)
        grows[3:4, :WIDTH] = jnp.sum(n2_grad, axis=0, keepdims=True)
        grows[4:5, :WIDTH] = sum(
            jnp.sum(dyall[l, piece(y, a), :].astype(F32), axis=0, keepdims=True) for a in PARTS
        )
        grows[6:7, :WIDTH] = jnp.sum(hidden_grad.astype(F32), axis=0, keepdims=True)
        joint_bias = jnp.sum(joint_grad.astype(F32), axis=0, keepdims=True)
        for h in range(4):

            @pl.when(y == h)
            def _():
                for i, (f, k) in enumerate(pieces_of(h)):
                    grows[7 + k : 8 + k, 48 * f : 48 * f + 48] = joint_bias[:, 48 * i : 48 * i + 48]

        keep(3, l, jnp.concatenate([grows[:, 48 * f : 48 * f + 128] for f in range(16)], axis=0))

    def backward_end(a, l):
        total = reduce_end(a, 1, l)
        values = xall[l, piece(y, a), :].astype(F32)
        center = values - jnp.mean(values, axis=-1, keepdims=True)
        scale = lax.rsqrt(jnp.mean(center * center, axis=-1, keepdims=True) + 1e-5)
        near = center * scale
        pulled = scale * (
            total
            - jnp.mean(total, axis=-1, keepdims=True)
            - near * jnp.mean(total * near, axis=-1, keepdims=True)
        )
        return (dyall[l, piece(y, a), :].astype(F32) + pulled).astype(BF16)

    def norm_back(l, hidden_grad, joint_grad):
        n1_grads, n2_grads = [], []
        for a in PARTS:
            rows = slice(a * SPLIT, (a + 1) * SPLIT)
            n1_grads.append(dot_nt(joint_grad[rows], wq[l]))
            n2_grads.append(dot_nt(hidden_grad[rows], we[l]))
            reduce_start(n1_grads[a] * vrows[l, 0:1, :] + n2_grads[a] * vrows[l, 2:3, :], a, 1, l)
        return jnp.concatenate(n1_grads, axis=0), jnp.concatenate(n2_grads, axis=0)

    forward(0)

    @pl.when(micro == 1)
    def _():
        gather_relay(1)

    for a in PARTS:
        middle = forward_end(a, 0)
        xall[1, piece(y, a), :] = middle
        share(xall.at[1], a, asend.at[0, 1], arecv.at[0, 1])
        staged[0, 0, HALF * a : HALF * (a + 1), :] = middle
    forward(1)

    hidden_grad = arrive_back(1)
    hidden_weights(1, hidden_grad)
    joint_grad = attention_back(1)
    n1_grad, n2_grad = norm_back(1, hidden_grad, joint_grad)
    keep(0, 1, dot_tn(n1s[1], joint_grad))
    for t in (2, 1, 4, 0):
        on_core(fold, t, 1)
    for a in PARTS:
        upper = backward_end(a, 1)
        dyall[0, piece(y, a), :] = upper
        share(dyall.at[0], a, asend.at[1, 0], arecv.at[1, 0])
        staged[1, 1, HALF * a : HALF * (a + 1), :] = upper
    vector_grads(1, hidden_grad, joint_grad, n1_grad, n2_grad)
    on_core(fold, 3, 1)
    for t in (2, 1, 0):
        on_core(relay, t, 1)
    for a in PARTS:
        staged[0, 1, HALF * a : HALF * (a + 1), :] = forward_end(a, 1)
    remote(staged.at[0, 1 - micro], lo_out.at[micro], osend.at[0], orecv.at[0], sibling).start()

    hidden_grad = arrive_back(0)
    hidden_weights(0, hidden_grad)
    joint_grad = attention_back(0)
    keep(0, 0, dot_tn(n1s[0], joint_grad))
    for t in (2, 1, 0, 4):
        on_core(fold, t, 0)
    for t in BACK:
        on_core(wide_end, t, 1)
    n1_grad, n2_grad = norm_back(0, hidden_grad, joint_grad)
    for t in (2, 1):
        on_core(relay, t, 0)
    vector_grads(0, hidden_grad, joint_grad, n1_grad, n2_grad)
    on_core(fold, 3, 0)
    for t in BACK:
        on_core(narrow_end, t, 1)
    on_core(relay, 0, 0)
    for a in PARTS:
        staged[1, 0, HALF * a : HALF * (a + 1), :] = backward_end(a, 0)
    remote(staged.at[1, 1 - micro], ig_out.at[micro], osend.at[1], orecv.at[1], sibling).start()
    lo_out[micro] = staged[0, micro]
    ig_out[micro] = staged[1, micro]
    for t in (4, 2, 1, 3, 0):
        on_core(wide_end, t, 0)
    for t in (4, 2, 1, 3, 0):
        on_core(narrow_end, t, 0)

    remote(end_e, out_e.at[y], ysend.at[1, 3], yrecv.at[1, 3], sibling).wait()
    for t in range(4):
        for k, d in enumerate(NEAR):
            src = outs[t].at[ring(y, 4 - d)]
            remote(src, src, ysend.at[t, k], yrecv.at[t, k], sibling).wait_recv()
            remote(src, src, ysend.at[t, k], yrecv.at[t, k], sibling).wait_send()
            remote(narrows[t].at[k], narrows[t].at[k], bsend.at[t, k], brecv.at[t, k], sibling).wait_send()
        for k in range(15):
            remote(slot(t, 0, 0), slot(t, 0, 0), gsend.at[t, k], grecv.at[t, 0], sibling).wait_send()
    for t in range(5):
        for k in range(6 if t < 3 else 3):
            src = wides[t].at[0, pl.ds(0, 2)] if t < 3 else wides[t].at[0]
            remote(src, src, wsend.at[t, k], wrecv.at[t, k], sibling).wait_send()
        remote(wholes[t].at[0], wholes[t].at[0], csend.at[t], crecv.at[t], sibling).wait_send()
        remote(helds[t], helds[t], hsend.at[t], hrecv.at[t], sibling).wait_send()

    @pl.when(holds)
    def _():
        for k in range(3):
            remote(out_d, out_d, ysend.at[4, k], yrecv.at[4, 0], sibling).wait_send()
            remote(band(0, 0), band(0, 0), dsend.at[k], drecv.at[0], sibling).wait_send()

    @pl.when(jnp.logical_not(holds))
    def _():
        remote(out_d, out_d, ysend.at[4, 0], yrecv.at[4, 0], sibling).wait_recv()
        remote(md, md, bsend.at[4, 0], brecv.at[4, 0], sibling).wait_send()

    for k in range(3):
        remote(band(0, 0), band(0, 0), dsend.at[3 + k], drecv.at[0], sibling).wait_send()
        for a in PARTS:
            src = posall.at[piece(y, a), :]
            remote(src, src, posend.at[a, k], porecv.at[a, k], sibling).wait_send()
            for l in range(2):
                for back in range(2):
                    src = xall.at[0, piece(y, a), :]
                    remote(src, src, asend.at[back, l, a, k], arecv.at[back, l, a, k], sibling).wait_send()
                    src = prec.at[back, l, a, k]
                    remote(src, src, rsend.at[back, l, a, k], rrecv.at[back, l, a, k], sibling).wait_send()
    for i, ref in enumerate((lo_out, ig_out)):
        remote(ref.at[0], ref.at[0], osend.at[i], orecv.at[i], sibling).wait()


def run_program(tokens, cot, positions, tables, vectors, weights):
    vmem = pl.BlockSpec(memory_space=pltpu.VMEM)
    hbm = pl.BlockSpec(memory_space=pl.ANY)
    dma = pltpu.SemaphoreType.DMA
    sizes = [(rows, cols) for rows, cols, _ in KINDS]

    def stacks(lead, dense_lead):
        return [pltpu.VMEM((*lead, rows, cols), BF16) for rows, cols in sizes] + [
            pltpu.VMEM((*dense_lead, 48, WIDTH), BF16)
        ]

    return pl.pallas_call(
        program_kernel,
        out_shape=[jax.ShapeDtypeStruct((4, rows, cols), BF16) for rows, cols in sizes]
        + [jax.ShapeDtypeStruct((48, WIDTH), BF16)]
        + [jax.ShapeDtypeStruct((2, TOK, WIDTH), BF16)] * 2,
        in_specs=[hbm, hbm, vmem, hbm] + [vmem] * 8 + [hbm] * 4,
        out_specs=[vmem] * 7,
        scratch_shapes=[
            pltpu.VMEM((6, LEN, 128), F32),
            pltpu.VMEM((48, 3 * WIDTH), BF16),
            pltpu.VMEM((48, 4 * WIDTH), BF16),
            pltpu.VMEM((48, 3 * GROUP), BF16),
            pltpu.VMEM((48, WIDTH), BF16),
            pltpu.VMEM((16, 128), BF16),
            pltpu.VMEM((16, 128), F32),
        ]
        + [pltpu.VMEM((2, 16 * rows, cols), BF16) for rows, cols in sizes]
        + [pltpu.VMEM((2, GROUP, WIDTH), BF16)]
        + stacks((2, 4, 4), (2, 4))
        + stacks((4, 4), (4,))
        + [pltpu.VMEM((2 if rows == 48 else 3, 4, rows, cols), BF16) for rows, cols in sizes]
        + [pltpu.VMEM((3, 48, WIDTH), BF16)]
        + [pltpu.VMEM((2, 2, rows, cols), BF16) for rows, cols in sizes[:3]] * 2
        + stacks((4,), ())
        + stacks((3,), (3,))
        + [
            pltpu.VMEM((2, LEN, WIDTH), BF16),
            pltpu.VMEM((2, LEN, WIDTH), BF16),
            pltpu.VMEM((LEN, 128), F32),
            pltpu.VMEM((2, 2, LEN, WIDTH), F32),
            pltpu.VMEM((2, 2, LEN, WIDTH), BF16),
            pltpu.VMEM((2, 2, 2, 3, HALF, WIDTH), BF16),
            pltpu.VMEM((2, LEN, 3 * GROUP), BF16),
            pltpu.VMEM((2, 3, LEN, LEN), F32),
            pltpu.VMEM((2, LEN, GROUP), BF16),
            pltpu.VMEM((2, LEN, WIDTH), BF16),
            pltpu.VMEM((2, LEN, WIDTH), F32),
            pltpu.VMEM((2, LEN, WIDTH), BF16),
            pltpu.VMEM((2, LEN, WIDTH), BF16),
            pltpu.VMEM((2, LEN, WIDTH), F32),
            pltpu.VMEM((2, 16, WIDTH), F32),
            pltpu.VMEM((2, 8, 3 * GROUP), F32),
            pltpu.VMEM((16, WIDTH + 128), F32),
            pltpu.VMEM((2, 2, TOK, WIDTH), BF16),
            pltpu.VMEM((48, WIDTH), BF16),
            dma((9,)),
            dma((4, 15)),
            dma((4, 16)),
            dma((6,)),
            dma((4,)),
            dma((5,)),
            dma((5,)),
            dma((2, 2, 2, 3)),
            dma((2, 2, 2, 3)),
            dma((2, 2, 2, 3)),
            dma((2, 2, 2, 3)),
            dma((2, 3)),
            dma((2, 3)),
            dma((5,)),
            dma((5,)),
            dma((5, 6)),
            dma((5, 6)),
            dma((5, 3)),
            dma((5, 3)),
            dma((5, 4)),
            dma((5, 4)),
            dma((2,)),
            dma((2,)),
        ],
        compiler_params=pltpu.CompilerParams(
            collective_id=1, has_side_effects=True, vmem_limit_bytes=58 * MIB
        ),
        name="layers",
    )(tokens, cot, positions, tables, *vectors, *weights)


def lay_out_kernel(
    q, e, s, v, d, lo, ig,
    lo_out, ig_out, o0, o1, o2, o3, q_out, qb_out, d_out, db_out, e_out, eb_out, s_out, sb_out,
):
    lo_out[...] = lo[...]
    ig_out[...] = ig[...]
    for t in range(3):
        for h in range(4):
            at = WIDTH * t + GROUP * h
            q_out[0, :, at : at + GROUP] = q[h, :, GROUP * t : GROUP * (t + 1)].astype(F32)
    for f in range(0, 16, 2):
        e_out[0, :, GROUP * f : GROUP * (f + 2)] = jnp.concatenate(
            [e[h, :, 48 * i : 48 * i + 48].astype(F32) for i in (f, f + 1) for h in range(4)], axis=1
        )
    for h in range(4):
        s_out[0, 48 * h : 48 * h + 48, :] = s[h].astype(F32)
    d_out[0] = d[...].astype(F32)
    total = v[0].astype(F32) + v[1].astype(F32) + v[2].astype(F32) + v[3].astype(F32)
    for i, ref in enumerate((o0, o1, o2, o3, db_out)):
        ref[...] = total[i : i + 1, 0:48]
    sb_out[...] = total[4:5, 0:48]
    qb_out[...] = jnp.concatenate([total[7 + k : 8 + k, 0:48] for k in range(3)], axis=1)
    eb_out[...] = jnp.concatenate([v[h].astype(F32)[6:7, 0:48] for h in range(4)], axis=1)


def lay_out(parts):
    vmem = pl.BlockSpec(memory_space=pltpu.VMEM)
    flat = jax.ShapeDtypeStruct((1, 48), F32)
    rows = jax.ShapeDtypeStruct((2, TOK, WIDTH), BF16)

    def wide(height, width):
        return jax.ShapeDtypeStruct((1, height, width), F32)

    shapes = [
        rows, rows, flat, flat, flat, flat, wide(48, 3 * WIDTH), jax.ShapeDtypeStruct((1, 144), F32),
        wide(48, WIDTH), flat, wide(48, 4 * WIDTH), jax.ShapeDtypeStruct((1, GROUP), F32),
        wide(GROUP, WIDTH), flat,
    ]
    return pl.pallas_call(
        lay_out_kernel,
        out_shape=shapes,
        in_specs=[vmem] * 7,
        out_specs=[vmem] * 14,
        compiler_params=pltpu.CompilerParams(vmem_limit_bytes=62 * MIB),
        name="lay_out",
    )(*parts)


def angle_tables():
    lane = np.arange(128) % HD
    frequency = np.exp(-math.log(10000.0) * (2.0 / ROT) * np.arange(ROT // 2)).astype(np.float32)
    tables = []
    for offset in (0, 1):
        row = np.arange(LEN)
        token = (row // HALF % 4) * TOK + row // SPLIT * HALF + row % HALF
        spots = (2 * token + offset).astype(np.float32)
        angle = (spots[:, None] * frequency[None, :])[:, lane % 8].astype(np.float64)
        cosine = np.where(lane < ROT, np.cos(angle), 1.0)
        low_sine = np.where(lane < 8, -np.sin(angle), 0.0)
        high_sine = np.where((lane >= 8) & (lane < ROT), np.sin(angle), 0.0)
        tables += [cosine, low_sine, high_sine]
    return np.stack(tables).astype(np.float32)


def on_device(
    tokens_in, cotangent, positions, first_gain, first_bias, second_gain, second_bias,
    qkv_weight, qkv_bias, dense_weight, dense_bias, expand_weight, expand_bias,
    shrink_weight, shrink_bias,
):
    parts = run_program(
        tokens_in,
        cotangent,
        positions,
        jnp.asarray(angle_tables()),
        (first_gain, first_bias, second_gain, second_bias, dense_bias, shrink_bias, qkv_bias, expand_bias),
        (qkv_weight, expand_weight, shrink_weight, dense_weight),
    )
    layer_out, input_grad, *rest = lay_out(parts)
    shape = (1, 2, 1, TOK, WIDTH)
    return (layer_out.reshape(shape), input_grad.reshape(shape), *rest)


def solution(mesh):
    tokens = P(None, "fsdp", "seq", None)
    flat = P("section", "fsdp")
    wide = P("section", "fsdp", None)
    out = P("section", None, "fsdp", "seq", None)
    return jax.shard_map(
        on_device,
        mesh=mesh,
        in_specs=(
            tokens, tokens, P(None, "fsdp", "seq"), flat, flat, flat, flat,
            wide, flat, wide, flat, wide, flat, wide, flat,
        ),
        out_specs=(
            out, out, flat, flat, flat, flat, wide, flat, wide, flat, wide, flat, wide, flat,
        ),
        check_vma=False,
    )
```
